128 devices in a mesh: row: 16 (over x, y), grp: 8 (over z, core).
Axes of the slice: x: 4, y: 4, z: 4, core: 2. Of those that a mesh axis runs over, the one named last changes fastest.
Arguments:
- node_feat: bfloat16 [131072, 256], P(('row', 'grp')), may hold values from -6 to 6
- edge_feat: bfloat16 [524288, 256], P(('row', 'grp')), may hold values from -6 to 6
- senders: int32 [524288], P(('row', 'grp')), may hold values from 0 to 1279, as said below
- receivers: int32 [524288], P(('row', 'grp')), may hold values from 0 to 1023
- edge_count: int32 [128], P(('row', 'grp')), may hold values from 1024 to 4096, as said below
- halo_index: int32 [128, 8, 32], P(('row', 'grp')), may hold values from 0 to 1023
- coarse_target: int32 [131072], P(('row', 'grp')), may hold values from 0 to 511, as said below
- restrict_weight: bfloat16 [131072], P(('row', 'grp')), may hold values from 0.25 to 1
- prolong_weight: bfloat16 [131072], P(('row', 'grp')), may hold values from 0.5 to 1.5
- edge_in: bfloat16 [768, 256], replicated, may hold values from -0.21875 to 0.21875
- edge_bias: bfloat16 [256], replicated, may hold values from -3 to 3
- edge_out: bfloat16 [256, 256], replicated, may hold values from -0.375 to 0.375
- node_in: bfloat16 [512, 256], replicated, may hold values from -0.25 to 0.25
- node_bias: bfloat16 [256], replicated, may hold values from -3 to 3
- node_out: bfloat16 [256, 256], replicated, may hold values from -0.375 to 0.375
- coarse_in: bfloat16 [256, 256], replicated, may hold values from -0.375 to 0.375
- coarse_bias: bfloat16 [256], replicated, may hold values from -3 to 3
- coarse_out: bfloat16 [256, 256], replicated, may hold values from -0.375 to 0.375
- prolong: bfloat16 [256, 256], replicated, may hold values from -0.375 to 0.375
- grad_nodes: bfloat16 [131072, 256], P(('row', 'grp')), may hold values from -6 to 6
- grad_edges: bfloat16 [524288, 256], P(('row', 'grp')), may hold values from -6 to 6
Outputs:
- node_result: float32 [131072, 256], P(('row', 'grp'))
- edge_new: float32 [524288, 256], P(('row', 'grp'))
- d_node_feat: float32 [131072, 256], P(('row', 'grp'))
- d_edge_feat: float32 [524288, 256], P(('row', 'grp'))
- d_edge_in: float32 [768, 256], replicated
- d_edge_bias: float32 [256], replicated
- d_edge_out: float32 [256, 256], replicated
- d_node_in: float32 [512, 256], replicated
- d_node_bias: float32 [256], replicated
- d_node_out: float32 [256, 256], replicated
- d_coarse_in: float32 [256, 256], replicated
- d_coarse_bias: float32 [256], replicated
- d_coarse_out: float32 [256, 256], replicated
- d_prolong: float32 [256, 256], replicated
The draws below stay inside these ranges and needn't reach their ends.
Inputs may be any that keep to these rules, and one draw needn't show every extreme that they name: `edge_count`: edge slots in use in each partition's padded block of 4096; some partition is full in every draw. Most senders are local rows; the others are halo slots. `coarse_target`: most fine nodes of a partition map into the 64 coarse rows that its grp index owns.
All inputs are finite; a program needn't handle non-finite values.
Results may differ from the reference program's by a relative error of at most 0.017.
Values may be sent and summed in bfloat16 or wider, within the bound.
A program may use at most 128 MiB of HBM per device.

```python
import jax
import jax.numpy as jnp

H = 256
NF_DEV = 1024
EF_DEV = 4096
SLOT = 32
NC_DEV = 64
NODES = 131072
EDGES = 524288
NX = 1280
GC = 512
COARSE = 8192
N_ROW = 16
N_GRP = 8
DEVICES = 128


def draw_edge_count(key, part):
    key = jax.random.fold_in(key, 11)
    key_counts, key_full = jax.random.split(key)
    counts = jax.random.randint(key_counts, (DEVICES,), EF_DEV // 4, EF_DEV + 1)
    full = jax.random.randint(key_full, (), 0, DEVICES)
    return jnp.where(jnp.arange(DEVICES) == full, EF_DEV, counts).astype(jnp.int32)


def draw_senders(key, part):
    key = jax.random.fold_in(key, 23)
    key_pick, key_local, key_halo = jax.random.split(key, 3)
    pick = jax.random.randint(key_pick, (EDGES,), 0, 100)
    local = jax.random.randint(key_local, (EDGES,), 0, NF_DEV)
    halo = jax.random.randint(key_halo, (EDGES,), NF_DEV, NX)
    return jnp.where(pick < 15, halo, local).astype(jnp.int32)


def draw_coarse_target(key, part):
    key = jax.random.fold_in(key, 37)
    key_pick, key_own, key_any = jax.random.split(key, 3)
    node_grp = jnp.arange(NODES, dtype=jnp.int32) // NF_DEV % N_GRP
    pick = jax.random.randint(key_pick, (NODES,), 0, 100)
    own = node_grp * NC_DEV + jax.random.randint(key_own, (NODES,), 0, NC_DEV)
    anywhere = jax.random.randint(key_any, (NODES,), 0, GC)
    return jnp.where(pick < 85, own, anywhere).astype(jnp.int32)


def touch_ends(values, stream_key, least, top_value):
    extent = values.shape
    spot = [jax.random.randint(jax.random.fold_in(stream_key, axis), (), 0, extent[axis]) for axis in range(len(extent))]
    values = values.at[tuple(spot)].set(least)
    longest = extent.index(max(extent))
    spot[longest] = (spot[longest] + 1) % extent[longest]
    return values.at[tuple(spot)].set(top_value)


def level_of(own_key, shape, pieces, least, top_value):
    level = 1.0
    for dim, shards_of in pieces:
        heights = jax.random.uniform(jax.random.fold_in(jax.random.fold_in(own_key, 6), dim), (shards_of,), jnp.float32, least / len(pieces), top_value / len(pieces))
        level = level * jnp.repeat(jnp.exp(heights), shape[dim] // shards_of).reshape((-1,) + (1,) * (len(shape) - 1 - dim))
    return level


def scatter_about(key, shape, spread, reach, cuts=(), held_as=jnp.bfloat16):
    drawn = jax.random.normal(key, shape, jnp.float32) * spread
    if len(cuts) > 0:
        drawn = level_of(key, shape, cuts, -0.22, 0.18) * drawn
    return jnp.clip(drawn, min=-reach, max=reach).astype(held_as)


def setup_inputs(seed: int = 0) -> dict:
    key_list = jax.random.split(jax.random.key(seed), 22)
    node_feat = scatter_about(key_list[0], (NODES, H), 1.0, 6.0, ((0, 128),))
    edge_feat = scatter_about(key_list[1], (EDGES, H), 1.0, 6.0, ((0, 128),))
    senders = draw_senders(jax.random.fold_in(key_list[21], 71), 0)
    receivers = touch_ends(jax.random.randint(key_list[3], (EDGES,), 0, NF_DEV), jax.random.fold_in(key_list[3], 1), 0, NF_DEV - 1).astype(jnp.int32)
    edge_count = draw_edge_count(jax.random.fold_in(key_list[21], 71), 0)
    halo_index = touch_ends(jax.random.randint(key_list[5], (DEVICES, 8, SLOT), 0, NF_DEV), jax.random.fold_in(key_list[5], 1), 0, NF_DEV - 1).astype(jnp.int32)
    coarse_target = draw_coarse_target(jax.random.fold_in(key_list[21], 71), 0)
    restrict_weight = jnp.clip(0.25 + 0.75 * jax.random.uniform(key_list[7], (NODES,), jnp.float32) ** level_of(key_list[7], (NODES,), ((0, 128),), -0.2, 0.2), 0.25, 1.0).astype(jnp.bfloat16)
    prolong_weight = jnp.clip(0.5 + 1.0 * jax.random.uniform(key_list[8], (NODES,), jnp.float32) ** level_of(key_list[8], (NODES,), ((0, 128),), -0.2, 0.2), 0.5, 1.5).astype(jnp.bfloat16)
    edge_in = scatter_about(key_list[9], (3 * H, H), (3 * H) ** -0.5, 0.21875)
    edge_bias = scatter_about(key_list[10], (H,), 0.5, 3.0)
    edge_out = scatter_about(key_list[11], (H, H), H ** -0.5, 0.375)
    node_in = scatter_about(key_list[12], (2 * H, H), (2 * H) ** -0.5, 0.25)
    node_bias = scatter_about(key_list[13], (H,), 0.5, 3.0)
    node_out = scatter_about(key_list[14], (H, H), H ** -0.5, 0.375)
    coarse_in = scatter_about(key_list[15], (H, H), H ** -0.5, 0.375)
    coarse_bias = scatter_about(key_list[16], (H,), 0.5, 3.0)
    coarse_out = scatter_about(key_list[17], (H, H), H ** -0.5, 0.375)
    prolong = scatter_about(key_list[18], (H, H), H ** -0.5, 0.375)
    grad_nodes = scatter_about(key_list[19], (NODES, H), 1.0, 6.0, ((0, 128),))
    grad_edges = scatter_about(key_list[20], (EDGES, H), 1.0, 6.0, ((0, 128),))
    return dict(node_feat=node_feat, edge_feat=edge_feat, senders=senders, receivers=receivers, edge_count=edge_count, halo_index=halo_index, coarse_target=coarse_target, restrict_weight=restrict_weight, prolong_weight=prolong_weight, edge_in=edge_in, edge_bias=edge_bias, edge_out=edge_out, node_in=node_in, node_bias=node_bias, node_out=node_out, coarse_in=coarse_in, coarse_bias=coarse_bias, coarse_out=coarse_out, prolong=prolong, grad_nodes=grad_nodes, grad_edges=grad_edges)


def matmul(a, b):
    return jnp.dot(a, b, preferred_element_type=jnp.float32)


def silu_slope(u):
    sg = jax.nn.sigmoid(u)
    return sg * (1.0 + u * (1.0 - sg))


def reference(node_feat, edge_feat, senders, receivers, edge_count, halo_index, coarse_target, restrict_weight, prolong_weight, edge_in, edge_bias, edge_out, node_in, node_bias, node_out, coarse_in, coarse_bias, coarse_out, prolong, grad_nodes, grad_edges):
    bf = jnp.bfloat16
    f32 = jnp.float32
    width = node_feat.shape[1]
    parts = jnp.arange(DEVICES, dtype=jnp.int32)
    part_row = (parts // N_GRP).astype(jnp.int32)
    part_grp = (parts % N_GRP).astype(jnp.int32)
    slots = jnp.arange(8 * SLOT, dtype=jnp.int32)
    direction = (slots // SLOT).astype(jnp.int32)
    within = (slots % SLOT).astype(jnp.int32)
    offset_row = jnp.array([-1, -1, -1, 0, 0, 1, 1, 1], dtype=jnp.int32)
    offset_grp = jnp.array([-1, 0, 1, -1, 1, -1, 0, 1], dtype=jnp.int32)
    source_row = part_row[:, None] - offset_row[direction][None, :]
    source_grp = part_grp[:, None] - offset_grp[direction][None, :]
    inside = (source_row >= 0) & (source_row < N_ROW) & (source_grp >= 0) & (source_grp < N_GRP)
    source_part = jnp.where(inside, source_row * N_GRP + source_grp, 0).astype(jnp.int32)
    halo_table = (source_part * NF_DEV + halo_index[source_part, direction[None, :], within[None, :]]).astype(jnp.int32)
    local_table = parts[:, None] * NF_DEV + jnp.arange(NF_DEV, dtype=jnp.int32)[None, :]
    ext_table = jnp.concatenate([local_table, halo_table], axis=1).astype(jnp.int32)
    presence = jnp.concatenate([jnp.ones((DEVICES, NF_DEV), f32), inside.astype(f32)], axis=1)
    edge_part = (jnp.arange(EDGES, dtype=jnp.int32) // EF_DEV).astype(jnp.int32)
    src = ext_table[edge_part, senders].astype(jnp.int32)
    present = presence[edge_part, senders][:, None]
    dst = (edge_part * NF_DEV + receivers).astype(jnp.int32)
    valid = ((jnp.arange(EDGES, dtype=jnp.int32) % EF_DEV) < edge_count[edge_part]).astype(f32)[:, None]
    node_part = (jnp.arange(NODES, dtype=jnp.int32) // NF_DEV).astype(jnp.int32)
    coarse_row = ((node_part // N_GRP) * GC + coarse_target).astype(jnp.int32)
    a_edge, a_send, a_recv = edge_in[:width], edge_in[width:2 * width], edge_in[2 * width:]
    c_node, c_agg = node_in[:width], node_in[width:]
    sent_rows = node_feat[src] * present.astype(bf)
    recv_rows = node_feat[dst]
    pre_edge = matmul(edge_feat, a_edge) + matmul(sent_rows, a_send) + matmul(recv_rows, a_recv) + edge_bias.astype(f32)
    hid_edge = jax.nn.silu(pre_edge).astype(bf)
    edge_new = edge_feat.astype(f32) + valid * matmul(hid_edge, edge_out)
    agg = jax.ops.segment_sum(valid * edge_new.astype(bf).astype(f32), dst, NODES).astype(bf)
    pre_node = matmul(node_feat, c_node) + matmul(agg, c_agg) + node_bias.astype(f32)
    hid_node = jax.nn.silu(pre_node).astype(bf)
    updated = node_feat.astype(f32) + matmul(hid_node, node_out)
    rweight = restrict_weight.astype(f32)[:, None]
    pweight = prolong_weight.astype(f32)[:, None]
    coarse = jax.ops.segment_sum(rweight * updated.astype(bf).astype(f32), coarse_row, COARSE)
    pre_coarse = matmul(coarse.astype(bf), coarse_in) + coarse_bias.astype(f32)
    hid_coarse = jax.nn.silu(pre_coarse).astype(bf)
    coarse_new = coarse + matmul(hid_coarse, coarse_out)
    q_rows = coarse_new.astype(bf)
    node_result = updated + pweight * matmul(q_rows[coarse_row], prolong)
    grad_z = grad_nodes.astype(f32)
    scaled = (pweight * grad_z).astype(bf)
    summed = jax.ops.segment_sum(scaled.astype(f32), coarse_row, COARSE)
    summed_b = summed.astype(bf)
    d_prolong = matmul(q_rows.T, summed_b)
    grad_cn = matmul(summed_b, prolong.T)
    grad_cnb = grad_cn.astype(bf)
    grad_uc = matmul(grad_cnb, coarse_out.T) * silu_slope(pre_coarse)
    grad_ucb = grad_uc.astype(bf)
    d_coarse_out = matmul(hid_coarse.T, grad_cnb)
    d_coarse_in = matmul(coarse.astype(bf).T, grad_ucb)
    d_coarse_bias = jnp.sum(grad_uc, axis=0)
    grad_c = grad_cn + matmul(grad_ucb, coarse_in.T)
    grad_y = grad_z + rweight * grad_c.astype(bf)[coarse_row].astype(f32)
    grad_yb = grad_y.astype(bf)
    grad_un = matmul(grad_yb, node_out.T) * silu_slope(pre_node)
    grad_unb = grad_un.astype(bf)
    d_node_out = matmul(hid_node.T, grad_yb)
    d_node_in = jnp.concatenate([matmul(node_feat.T, grad_unb), matmul(agg.T, grad_unb)], axis=0)
    d_node_bias = jnp.sum(grad_un, axis=0)
    grad_agg = matmul(grad_unb, c_agg.T).astype(bf)
    grad_en = grad_edges.astype(f32) + valid * grad_agg[dst].astype(f32)
    grad_mb = (valid * grad_en).astype(bf)
    grad_ue = matmul(grad_mb, edge_out.T) * silu_slope(pre_edge)
    grad_ueb = grad_ue.astype(bf)
    d_edge_out = matmul(hid_edge.T, grad_mb)
    d_edge_in = jnp.concatenate([matmul(edge_feat.T, grad_ueb), matmul(sent_rows.T, grad_ueb), matmul(recv_rows.T, grad_ueb)], axis=0)
    d_edge_bias = jnp.sum(grad_ue, axis=0)
    d_edge_feat = grad_en + matmul(grad_ueb, a_edge.T)
    grad_send = matmul(grad_ueb, a_send.T).astype(bf).astype(f32) * present
    grad_recv = matmul(grad_ueb, a_recv.T).astype(bf).astype(f32)
    d_node_feat = grad_y + matmul(grad_unb, c_node.T) + jax.ops.segment_sum(grad_recv, dst, NODES) + jax.ops.segment_sum(grad_send, src, NODES)
    return (node_result, edge_new, d_node_feat, d_edge_feat, d_edge_in, d_edge_bias, d_edge_out, d_node_in, d_node_bias, d_node_out, d_coarse_in, d_coarse_bias, d_coarse_out, d_prolong)
```

```python
import jax
import jax.numpy as jnp
from jax import lax
from jax.experimental import pallas as pl
from jax.experimental.pallas import tpu as pltpu
from jax.sharding import PartitionSpec as P

BF = jnp.bfloat16
F32 = jnp.float32
I32 = jnp.int32
MESH = pl.DeviceIdType.MESH
OFFSETS = ((-1, -1), (-1, 0), (-1, 1), (0, -1), (0, 1), (1, -1), (1, 0), (1, 1))
NR, NG = 16, 8
H = 256
NF = 1024
EF = 4096
NX = 1280
NT = NX + NF
GC = 512
NC = 64
BLK = 1024
SUB = 512
MIB = 1024 * 1024


def mm(a, b):
    return lax.dot_general(a, b, (((1,), (0,)), ((), ())), preferred_element_type=F32)


def mm_nt(a, b):
    return lax.dot_general(a, b, (((1,), (1,)), ((), ())), preferred_element_type=F32)


def mm_tn(a, b):
    return lax.dot_general(a, b, (((0,), (0,)), ((), ())), preferred_element_type=F32)


def silu_parts(u):
    sg = jax.nn.sigmoid(u)
    return u * sg, sg * (1.0 + u * (1.0 - sg))


def hot_rows(idx, lo, count, weight=None):
    parts = []
    for j in range(idx.shape[0]):
        place = lax.broadcasted_iota(I32, (count, 128), 0) + lo
        value = 1.0 if weight is None else weight[j : j + 1, :]
        parts.append(jnp.where(place == idx[j : j + 1, :], value, 0.0).astype(BF))
    return jnp.concatenate(parts, axis=1)


def hot_cols(idx_t, lo, count, weight_t=None):
    parts = []
    for j in range(idx_t.shape[1]):
        place = lax.broadcasted_iota(I32, (128, count), 1) + lo
        value = 1.0 if weight_t is None else weight_t[:, j : j + 1]
        parts.append(jnp.where(place == idx_t[:, j : j + 1], value, 0.0).astype(BF))
    return jnp.concatenate(parts, axis=0)


def halo_columns(hidx):
    wide = hidx.astype(F32)
    eye = lax.broadcasted_iota(I32, (32, 32), 0) == lax.broadcasted_iota(I32, (32, 32), 1)
    return [
        jnp.sum(jnp.where(eye, wide[d : d + 1, :], 0.0), axis=1, keepdims=True) for d in range(8)
    ]


def here():
    return lax.axis_index("row"), lax.axis_index("grp")


def shifted(r, g, dr, dg):
    return lax.rem(r + dr + NR, NR), lax.rem(g + dg + NG, NG)


def inside(r, g, dr, dg):
    rr, gg = r + dr, g + dg
    return (rr >= 0) & (rr < NR) & (gg >= 0) & (gg < NG)


def greet(r, g, steps):
    barrier = pltpu.get_barrier_semaphore()
    for dr, dg in steps:
        pl.semaphore_signal(
            barrier, inc=1, device_id=shifted(r, g, dr, dg), device_id_type=MESH
        )
    return lambda: pl.semaphore_wait(barrier, len(steps))


def over(n, fn):
    def step(k, carry):
        fn(k)
        return carry

    lax.fori_loop(1, n, step, 0)


def remote(src, dst, send, recv, place):
    return pltpu.make_async_remote_copy(
        src_ref=src, dst_ref=dst, send_sem=send, recv_sem=recv, device_id=place, device_id_type=MESH
    )


def rows(start, size):
    return pl.ds(pl.multiple_of(start * size, size), size)


GRP_STEPS = [(0, k) for k in range(1, NG)]
ROW_STEPS = [(k, 0) for k in range(1, NR)]
NEAR_STEPS = [(dr, dg) for dr, dg in OFFSETS]
HALO_PEERS = GRP_STEPS + [s for s in NEAR_STEPS if s[0] != 0]
ALL_PEERS = GRP_STEPS + ROW_STEPS + [s for s in NEAR_STEPS if s[0] != 0 and s[1] != 0]


def scatter_grp(r, g, part, land, send, recv, size):
    def copy(k):
        t = lax.rem(g + k, NG)
        return remote(part.at[rows(t, size)], land.at[k - 1], send.at[k - 1], recv.at[k - 1], (r, t))

    return copy


def halo_kernel(nf, hidx, ct, pw, gz, ein, p_out, halo_out, s_out, own, land, part, sland,
                hs, hr, ss, sr):
    r, g = here()
    ready = greet(r, g, HALO_PEERS)
    pick = jnp.concatenate(
        [
            jnp.where(lax.broadcasted_iota(I32, (32, NF), 1).astype(F32) == c, 1.0, 0.0).astype(BF)
            for c in halo_columns(hidx[...])
        ],
        axis=0,
    )
    own[...] = mm(pick, nf[...]).astype(BF)
    ready()
    halo = [
        remote(
            own.at[pl.ds(32 * d, 32)], land.at[pl.ds(32 * d, 32)], hs.at[d], hr.at[d],
            shifted(r, g, dr, dg),
        )
        for d, (dr, dg) in enumerate(OFFSETS)
    ]
    for c in halo:
        c.start()
    part[...] = mm(hot_rows(ct[...], 0, GC, pw[...].astype(F32)), gz[...]).astype(BF)
    scat = scatter_grp(r, g, part, sland, ss, sr, NC)
    over(NG, lambda k: scat(k).start())
    p_out[0:NF] = mm(nf[...], ein[H : 2 * H]).astype(BF)
    p_out[NX:] = mm(nf[...], ein[2 * H :]).astype(BF)
    for c in halo:
        c.wait()
    for d, (dr, dg) in enumerate(OFFSETS):
        got = land[32 * d : 32 * d + 32]
        halo_out[32 * d : 32 * d + 32] = jnp.where(inside(r, g, -dr, -dg), got, jnp.zeros_like(got))
    p_out[NF:NX] = mm(halo_out[...], ein[H : 2 * H]).astype(BF)
    over(NG, lambda k: scat(k).wait())
    total = part[rows(g, NC)].astype(F32)
    for k in range(NG - 1):
        total += sland[k].astype(F32)
    s_out[...] = total.astype(BF)


def mask_of(count, start, size):
    place = lax.broadcasted_iota(I32, (size, 1), 0) + start
    return jnp.where(place < count, 1.0, 0.0)


def edge_forward_kernel(count, ef, snd, rcv, ptab, ein, ebias, eout, en_out, he_out, ds_out, agg_out,
                        acc):
    step = pl.program_id(0)

    @pl.when(step == 0)
    def _():
        acc[...] = jnp.zeros_like(acc)

    snd_t = jnp.transpose(snd[...])
    rcv_t = jnp.transpose(rcv[...])
    bias = ebias[...].astype(F32)
    per = SUB // 128
    for h in range(BLK // SUB):
        at = slice(h * SUB, (h + 1) * SUB)
        lanes = slice(h * per, (h + 1) * per)
        x = ef[at]
        u = mm(x, ein[0:H]) + bias
        u += mm(hot_cols(snd_t[:, lanes], 0, NX), ptab[0:NX])
        u += mm(hot_cols(rcv_t[:, lanes], 0, NF), ptab[NX:])
        s, slope = silu_parts(u)
        he = s.astype(BF)
        he_out[at] = he
        ds_out[at] = slope.astype(BF)
        m = mask_of(count[0], step * BLK + h * SUB, SUB)
        new = x.astype(F32) + m * mm(he, eout[...])
        en_out[at] = new
        acc[...] += mm(hot_rows(rcv[lanes], 0, NF), (m * new).astype(BF))

    @pl.when(step == pl.num_programs(0) - 1)
    def _():
        agg_out[...] = acc[...].astype(BF)


def coarse_kernel(nf, agg, nin, nbias, nout, ct, rw, s_in, cin, cbias, cout, prol,
                  y_out, hn_out, dsn_out, gc_out, q_out, wc_out, cb_out,
                  part, land, gc_own, ss, sr, gs, gr):
    r, g = here()
    ready = greet(r, g, GRP_STEPS)
    un = mm(nf[...], nin[0:H]) + mm(agg[...], nin[H:]) + nbias[...].astype(F32)
    s, slope = silu_parts(un)
    hn = s.astype(BF)
    hn_out[...] = hn
    dsn_out[...] = slope.astype(BF)
    y = nf[...].astype(F32) + mm(hn, nout[...])
    y_out[...] = y
    part[...] = mm(hot_rows(ct[...], 0, GC, rw[...].astype(F32)), y.astype(BF)).astype(BF)
    ready()
    scat = scatter_grp(r, g, part, land, ss, sr, NC)
    over(NG, lambda k: scat(k).start())
    sb = s_in[...]
    gcn = mm_nt(sb, prol[...])
    gcnb = gcn.astype(BF)
    gh = mm_nt(gcnb, cout[...])
    over(NG, lambda k: scat(k).wait())
    c = part[rows(g, NC)].astype(F32)
    for k in range(NG - 1):
        c += land[k].astype(F32)
    cb = c.astype(BF)
    uc = mm(cb, cin[...]) + cbias[...].astype(F32)
    s, slope = silu_parts(uc)
    hc = s.astype(BF)
    guc = gh * slope
    gucb = guc.astype(BF)
    gc = (gcn + mm_nt(gucb, cin[...])).astype(BF)
    gc_own[...] = gc
    gc_out[rows(g, NC)] = gc

    def gather(k):
        return remote(
            gc_own, gc_out.at[rows(g, NC)], gs.at[k - 1], gr.at[k - 1], (r, lax.rem(g + k, NG))
        )

    over(NG, lambda k: gather(k).start())
    q = (c + mm(hc, cout[...])).astype(BF)
    q_out[...] = q
    wc_out[0:H] = mm_tn(cb, gucb).astype(BF)
    wc_out[H : 2 * H] = mm_tn(hc, gcnb).astype(BF)
    wc_out[2 * H :] = mm_tn(q, sb).astype(BF)
    cb_out[...] = jnp.sum(guc, axis=0, keepdims=True)
    over(NG, lambda k: gather(k).wait())


def backward_kernel(count, ef, ge, snd, rcv, he, ds, nf, agg, gz, hn, dsn, gc, ct, rw, halo,
                    ein, eout, nin, nout,
                    def_out, wl_out, wn_out, b_out, dn_out, dh_out,
                    gagg, gyn, ssum, wacc, bacc):
    step = pl.program_id(0)

    @pl.when(step == 0)
    def _():
        ssum[...] = jnp.zeros_like(ssum)
        wacc[...] = jnp.zeros_like(wacc)
        bacc[...] = jnp.zeros_like(bacc)
        table = hot_cols(jnp.transpose(ct[...]), 0, GC, jnp.transpose(rw[...].astype(F32)))
        gy = gz[...].astype(F32) + mm(table, gc[...])
        gyb = gy.astype(BF)
        gun = mm_nt(gyb, nout[...]) * dsn[...].astype(F32)
        gunb = gun.astype(BF)
        gagg[...] = mm_nt(gunb, nin[H:]).astype(BF)
        gyn[...] = gy + mm_nt(gunb, nin[0:H])
        wn_out[0:H] = mm_tn(nf[...], gunb).astype(BF)
        wn_out[H : 2 * H] = mm_tn(agg[...], gunb).astype(BF)
        wn_out[2 * H :] = mm_tn(hn[...], gyb).astype(BF)
        bacc[1:2] = jnp.sum(gun, axis=0, keepdims=True)

    rcv_t = jnp.transpose(rcv[...])
    per = SUB // 128
    for h in range(BLK // SUB):
        at = slice(h * SUB, (h + 1) * SUB)
        lanes = slice(h * per, (h + 1) * per)
        m = mask_of(count[0], step * BLK + h * SUB, SUB)
        gen = ge[at].astype(F32) + m * mm(hot_cols(rcv_t[:, lanes], 0, NF), gagg[...])
        gm = (m * gen).astype(BF)
        gue = mm_nt(gm, eout[...]) * ds[at].astype(F32)
        gueb = gue.astype(BF)
        def_out[at] = gen + mm_nt(gueb, ein[0:H])
        wacc[0:H] += mm_tn(ef[at], gueb)
        wacc[H:] += mm_tn(he[at], gm)
        bacc[0:1] += jnp.sum(gue, axis=0, keepdims=True)
        ssum[0:NX] += mm(hot_rows(snd[lanes], 0, NX), gueb)
        ssum[NX:] += mm(hot_rows(rcv[lanes], 0, NF), gueb)

    @pl.when(step == pl.num_programs(0) - 1)
    def _():
        sb = ssum[...].astype(BF)
        send_grad = mm_nt(sb[0:NX], ein[H : 2 * H])
        dh_out[...] = send_grad[NF:].astype(BF)
        dn_out[...] = gyn[...] + send_grad[0:NF] + mm_nt(sb[NX:], ein[2 * H :])
        wl_out[0:H] = wacc[0:H].astype(BF)
        wl_out[H : 2 * H] = (mm_tn(nf[...], sb[0:NF]) + mm_tn(halo[...], sb[NF:NX])).astype(BF)
        wl_out[2 * H : 3 * H] = mm_tn(nf[...], sb[NX:]).astype(BF)
        wl_out[3 * H :] = wacc[H:].astype(BF)
        b_out[...] = bacc[...]


ROWS_A, ROWS_B = 1536, 1024
WROWS = ROWS_A + ROWS_B
RA, RB = ROWS_A // NG, ROWS_B // NR


def half(p):
    return pl.ds(pl.multiple_of(lax.rem(p, 2) * 128, 128), 128)


def sum_kernel(wl, wn, wc, b_in, cb_in, dh, q_in,
               w_out, b_out, q_out, h_out,
               wbuf, a1, b1, accA, accB, a2, b2, pa, pb, gA, gB, bias0, bias1, bl1, bl2, land,
               hs, hr, qs, qr, a1s, a1r, b1s, b1r, a2s, a2r, b2s, b2r, a3s, a3r, b3s, b3r,
               a4s, a4r, b4s, b4r, c1s, c1r, c2s, c2r):
    r, g = here()
    ready = greet(r, g, ALL_PEERS)
    wbuf[0:1024] = wl[...]
    wbuf[1024:1792] = wn[...]
    wbuf[1792:2560] = wc[...]
    bias0[...] = b_in[...]
    bias0[2:3] = cb_in[...]
    ready()

    def grp(k):
        return (r, lax.rem(g + k, NG))

    def row(k):
        return (lax.rem(r + k, NR), g)

    halo = [
        remote(
            dh.at[pl.ds(32 * d, 32)], land.at[pl.ds(32 * d, 32)], hs.at[d], hr.at[d],
            shifted(r, g, -dr, -dg),
        )
        for d, (dr, dg) in enumerate(OFFSETS)
    ]
    for c in halo:
        c.start()

    def s1a(k):
        t = lax.rem(g + k, NG)
        return remote(wbuf.at[rows(t, RA)], a1.at[k - 1], a1s.at[k - 1], a1r.at[k - 1], (r, t))

    def s1b(k):
        t = lax.rem(r + k, NR)
        src = wbuf.at[pl.ds(pl.multiple_of(ROWS_A + t * RB, RB), RB)]
        return remote(src, b1.at[k - 1], b1s.at[k - 1], b1r.at[k - 1], (t, g))

    def c1(k):
        return remote(bias0, bl1.at[k - 1], c1s.at[k - 1], c1r.at[k - 1], grp(k))

    def c2(k):
        return remote(bias1, bl2.at[k - 1], c2s.at[k - 1], c2r.at[k - 1], row(k))

    def gq(k):
        return remote(q_in, q_out.at[rows(g, NC)], qs.at[k - 1], qr.at[k - 1], grp(k))

    over(NR, lambda k: s1b(k).start())
    over(NG, lambda k: s1a(k).start())
    over(NG, lambda k: c1(k).start())
    over(NG, lambda k: gq(k).start())
    q_out[rows(g, NC)] = q_in[...]

    PA, PB = RA // 8, RB // 4

    def s2a(k):
        t = lax.rem(r + k, NR)
        src = accA.at[rows(t // 2, PA), half(t)]
        return remote(src, a2.at[k - 1], a2s.at[k - 1], a2r.at[k - 1], (t, g))

    def s2b(k):
        t = lax.rem(g + k, NG)
        src = accB.at[rows(t // 2, PB), half(t)]
        return remote(src, b2.at[k - 1], b2s.at[k - 1], b2r.at[k - 1], (r, t))

    over(NR, lambda k: s1b(k).wait())
    total = wbuf[pl.ds(pl.multiple_of(ROWS_A + r * RB, RB), RB)].astype(F32)
    for k in range(NR - 1):
        total += b1[k].astype(F32)
    accB[...] = total
    over(NG, lambda k: s2b(k).start())

    over(NG, lambda k: s1a(k).wait())
    total = wbuf[rows(g, RA)].astype(F32)
    for k in range(NG - 1):
        total += a1[k].astype(F32)
    accA[...] = total
    over(NR, lambda k: s2a(k).start())

    over(NG, lambda k: c1(k).wait())
    total = bias0[...]
    for k in range(NG - 1):
        total += bl1[k]
    bias1[...] = total
    over(NR, lambda k: c2(k).start())

    def s3a(k):
        dst = gA.at[rows(r // 2, PA), half(r)]
        return remote(pa, dst, a3s.at[k - 1], a3r.at[k - 1], row(k))

    def s3b(k):
        dst = gB.at[rows(g // 2, PB), half(g)]
        return remote(pb, dst, b3s.at[k - 1], b3r.at[k - 1], grp(k))

    over(NG, lambda k: s2b(k).wait())
    total = accB[rows(g // 2, PB), half(g)]
    for k in range(NG - 1):
        total += b2[k]
    pb[...] = total
    gB[rows(g // 2, PB), half(g)] = total
    over(NG, lambda k: s3b(k).start())

    over(NR, lambda k: s2a(k).wait())
    total = accA[rows(r // 2, PA), half(r)]
    for k in range(NR - 1):
        total += a2[k]
    pa[...] = total
    gA[rows(r // 2, PA), half(r)] = total
    over(NR, lambda k: s3a(k).start())

    def s4a(k):
        at = w_out.at[rows(g, RA)]
        return remote(at, at, a4s.at[k - 1], a4r.at[k - 1], grp(k))

    def s4b(k):
        at = w_out.at[pl.ds(pl.multiple_of(ROWS_A + r * RB, RB), RB)]
        return remote(at, at, b4s.at[k - 1], b4r.at[k - 1], row(k))

    over(NG, lambda k: s3b(k).wait())
    w_out[pl.ds(pl.multiple_of(ROWS_A + r * RB, RB), RB)] = gB[...].astype(BF)
    over(NR, lambda k: s4b(k).start())

    over(NR, lambda k: s3a(k).wait())
    w_out[rows(g, RA)] = gA[...].astype(BF)
    over(NG, lambda k: s4a(k).start())

    for c in halo:
        c.wait()
    for d, (dr, dg) in enumerate(OFFSETS):
        got = land[32 * d : 32 * d + 32]
        h_out[32 * d : 32 * d + 32] = jnp.where(inside(r, g, dr, dg), got, jnp.zeros_like(got))
    over(NG, lambda k: gq(k).wait())
    over(NR, lambda k: c2(k).wait())
    total = bias1[...]
    for k in range(NR - 1):
        total += bl2[k]
    b_out[...] = total
    over(NR, lambda k: s4b(k).wait())
    over(NG, lambda k: s4a(k).wait())


def result_kernel(w, b, q, back, dn, y, ct, pw, hidx, prol,
                  nr_out, dnf_out, o_ein, o_eb, o_eout, o_nin, o_nb, o_nout, o_cin, o_cb, o_cout, o_pr):
    table = hot_cols(jnp.transpose(ct[...]), 0, GC, jnp.transpose(pw[...].astype(F32)))
    nr_out[...] = y[...] + mm(table, mm(q[...], prol[...]).astype(BF))
    pick = jnp.concatenate(
        [
            jnp.where(lax.broadcasted_iota(I32, (32, NF), 1).astype(F32) == c, 1.0, 0.0).astype(BF)
            for c in halo_columns(hidx[...])
        ],
        axis=0,
    )
    dnf_out[...] = dn[...] + mm_tn(pick, back[...])
    o_ein[...] = w[0:768].astype(F32)
    o_eout[...] = w[768:1024].astype(F32)
    o_nin[...] = w[1024:1536].astype(F32)
    o_nout[...] = w[1536:1792].astype(F32)
    o_cin[...] = w[1792:2048].astype(F32)
    o_cout[...] = w[2048:2304].astype(F32)
    o_pr[...] = w[2304:2560].astype(F32)
    o_eb[...] = b[0:1]
    o_nb[...] = b[1:2]
    o_cb[...] = b[2:3]


def body(node_feat, edge_feat, senders, receivers, edge_count, halo_index, coarse_target,
         restrict_weight, prolong_weight, edge_in, edge_bias, edge_out, node_in, node_bias, node_out,
         coarse_in, coarse_bias, coarse_out, prolong, grad_nodes, grad_edges):
    snd = senders.reshape(EF // 128, 128)
    rcv = receivers.reshape(EF // 128, 128)
    ct = coarse_target.reshape(NF // 128, 128)
    rw = restrict_weight.reshape(NF // 128, 128)
    pw = prolong_weight.reshape(NF // 128, 128)
    hidx = halo_index.reshape(8, 32)
    ebias, nbias, cbias = (v.reshape(1, H) for v in (edge_bias, node_bias, coarse_bias))

    def shape(dims, dtype=BF):
        return jax.ShapeDtypeStruct(dims, dtype)

    def sems(*sizes):
        return [pltpu.SemaphoreType.DMA((n,)) for n in sizes]

    def whole(n):
        return [pl.BlockSpec(memory_space=pltpu.VMEM)] * n

    smem = pl.BlockSpec(memory_space=pltpu.SMEM)

    def comm(ident, limit):
        return pltpu.CompilerParams(
            collective_id=ident, has_side_effects=True, vmem_limit_bytes=limit * MIB
        )

    ptab, halo, s_own = pl.pallas_call(
        halo_kernel,
        out_shape=[shape((NT, H)), shape((256, H)), shape((NC, H))],
        in_specs=whole(6),
        out_specs=whole(3),
        scratch_shapes=[
            pltpu.VMEM((256, H), BF),
            pltpu.VMEM((256, H), BF),
            pltpu.VMEM((GC, H), BF),
            pltpu.VMEM((NG - 1, NC, H), BF),
        ]
        + sems(8, 8, NG - 1, NG - 1),
        compiler_params=comm(0, 40),
        name="halo",
    )(node_feat, hidx, ct, pw, grad_nodes, edge_in)

    blocks = EF // BLK

    def by_edge(width=H):
        return pl.BlockSpec((BLK, width), lambda i: (i, 0))

    def fixed(dims):
        return pl.BlockSpec(dims, lambda i: (0, 0))

    idx_spec = pl.BlockSpec((BLK // 128, 128), lambda i: (i, 0))
    edge_new, he, ds, agg = pl.pallas_call(
        edge_forward_kernel,
        grid=(blocks,),
        out_shape=[shape((EF, H), F32), shape((EF, H)), shape((EF, H)), shape((NF, H))],
        in_specs=[
            smem, by_edge(), idx_spec, idx_spec, fixed((NT, H)), fixed((768, H)), fixed((1, H)),
            fixed((H, H)),
        ],
        out_specs=[by_edge(), by_edge(), by_edge(), fixed((NF, H))],
        scratch_shapes=[pltpu.VMEM((NF, H), F32)],
        compiler_params=pltpu.CompilerParams(
            dimension_semantics=("arbitrary",), vmem_limit_bytes=56 * MIB
        ),
        name="edge_forward",
    )(edge_count, edge_feat, snd, rcv, ptab, edge_in, ebias, edge_out)

    y, hn, dsn, gc, q, wc, cb = pl.pallas_call(
        coarse_kernel,
        out_shape=[
            shape((NF, H), F32), shape((NF, H)), shape((NF, H)), shape((GC, H)), shape((NC, H)),
            shape((768, H)), shape((1, H), F32),
        ],
        in_specs=whole(12),
        out_specs=whole(7),
        scratch_shapes=[
            pltpu.VMEM((GC, H), BF),
            pltpu.VMEM((NG - 1, NC, H), BF),
            pltpu.VMEM((NC, H), BF),
        ]
        + sems(*[NG - 1] * 4),
        compiler_params=comm(1, 40),
        name="coarse",
    )(node_feat, agg, node_in, nbias, node_out, ct, rw, s_own, coarse_in, cbias, coarse_out, prolong)

    d_edge_feat, wl, wn, bias, dn, dh = pl.pallas_call(
        backward_kernel,
        grid=(blocks,),
        out_shape=[
            shape((EF, H), F32), shape((1024, H)), shape((768, H)), shape((8, H), F32),
            shape((NF, H), F32), shape((256, H)),
        ],
        in_specs=[
            smem, by_edge(), by_edge(), idx_spec, idx_spec, by_edge(), by_edge(),
            fixed((NF, H)), fixed((NF, H)), fixed((NF, H)), fixed((NF, H)), fixed((NF, H)),
            fixed((GC, H)), fixed((8, 128)), fixed((8, 128)), fixed((256, H)),
            fixed((768, H)), fixed((H, H)), fixed((512, H)), fixed((H, H)),
        ],
        out_specs=[
            by_edge(), fixed((1024, H)), fixed((768, H)), fixed((8, H)), fixed((NF, H)), fixed((256, H)),
        ],
        scratch_shapes=[
            pltpu.VMEM((NF, H), BF),
            pltpu.VMEM((NF, H), F32),
            pltpu.VMEM((NT, H), F32),
            pltpu.VMEM((512, H), F32),
            pltpu.VMEM((8, H), F32),
        ],
        compiler_params=pltpu.CompilerParams(
            dimension_semantics=("arbitrary",), vmem_limit_bytes=56 * MIB
        ),
        name="backward",
    )(edge_count, edge_feat, grad_edges, snd, rcv, he, ds, node_feat, agg, grad_nodes, hn, dsn, gc, ct,
      rw, halo, edge_in, edge_out, node_in, node_out)

    w_all, b_all, q_all, back = pl.pallas_call(
        sum_kernel,
        out_shape=[shape((WROWS, H)), shape((8, H), F32), shape((GC, H)), shape((256, H))],
        in_specs=whole(7),
        out_specs=whole(4),
        scratch_shapes=[
            pltpu.VMEM((WROWS, H), BF),
            pltpu.VMEM((NG - 1, RA, H), BF),
            pltpu.VMEM((NR - 1, RB, H), BF),
            pltpu.VMEM((RA, H), F32),
            pltpu.VMEM((RB, H), F32),
            pltpu.VMEM((NR - 1, RA // 8, 128), F32),
            pltpu.VMEM((NG - 1, RB // 4, 128), F32),
            pltpu.VMEM((RA // 8, 128), F32),
            pltpu.VMEM((RB // 4, 128), F32),
            pltpu.VMEM((RA, H), F32),
            pltpu.VMEM((RB, H), F32),
            pltpu.VMEM((8, H), F32),
            pltpu.VMEM((8, H), F32),
            pltpu.VMEM((NG - 1, 8, H), F32),
            pltpu.VMEM((NR - 1, 8, H), F32),
            pltpu.VMEM((256, H), BF),
        ]
        + sems(8, 8, 7, 7, 7, 7, 15, 15, 15, 15, 7, 7, 15, 15, 7, 7, 7, 7, 15, 15, 7, 7, 15, 15),
        compiler_params=comm(2, 40),
        name="sums",
    )(wl, wn, wc, bias, cb, dh, q)

    outs = pl.pallas_call(
        result_kernel,
        out_shape=[
            shape((NF, H), F32), shape((NF, H), F32), shape((768, H), F32), shape((1, H), F32),
            shape((H, H), F32), shape((512, H), F32), shape((1, H), F32), shape((H, H), F32),
            shape((H, H), F32), shape((1, H), F32), shape((H, H), F32), shape((H, H), F32),
        ],
        in_specs=whole(10),
        out_specs=whole(12),
        compiler_params=pltpu.CompilerParams(vmem_limit_bytes=40 * MIB),
        name="results",
    )(w_all, b_all, q_all, back, dn, y, ct, pw, hidx, prolong)
    node_result, d_node_feat = outs[:2]
    grads = [o.reshape(H) if o.shape[0] == 1 else o for o in outs[2:]]
    return (node_result, edge_new, d_node_feat, d_edge_feat, *grads)


def solution(mesh):
    wide = P(("row", "grp"), None)
    line = P(("row", "grp"))
    in_specs = (
        (wide, wide, line, line, line, P(("row", "grp"), None, None), line, line, line)
        + (P(),) * 10
        + (wide, wide)
    )
    out_specs = (wide,) * 4 + (P(),) * 10
    return jax.shard_map(body, mesh=mesh, in_specs=in_specs, out_specs=out_specs, check_vma=False)
```

```python
import jax
import jax.numpy as jnp
from jax import lax
from jax.experimental import pallas as pl
from jax.experimental.pallas import tpu as pltpu
from jax.sharding import PartitionSpec as P

BF = jnp.bfloat16
F32 = jnp.float32
I32 = jnp.int32
MESH = pl.DeviceIdType.MESH
OFFSETS = ((-1, -1), (-1, 0), (-1, 1), (0, -1), (0, 1), (1, -1), (1, 0), (1, 1))
NR, NG = 16, 8
H = 256
NF = 1024
EF = 4096
NX = 1280
NT = NX + NF
GC = 512
NC = 64
BLK = 1024
SUB = 512
MIB = 1024 * 1024
LIMIT = 60


def mm(a, b):
    return lax.dot_general(a, b, (((1,), (0,)), ((), ())), preferred_element_type=F32)


def mm_nt(a, b):
    return lax.dot_general(a, b, (((1,), (1,)), ((), ())), preferred_element_type=F32)


def mm_tn(a, b):
    return lax.dot_general(a, b, (((0,), (0,)), ((), ())), preferred_element_type=F32)


def silu_parts(u):
    sg = jax.nn.sigmoid(u)
    return u * sg, sg * (1.0 + u * (1.0 - sg))


def hot_rows(idx, lo, count, weight=None):
    parts = []
    for j in range(idx.shape[0]):
        place = lax.broadcasted_iota(I32, (count, 128), 0) + lo
        value = 1.0 if weight is None else weight[j : j + 1, :]
        parts.append(jnp.where(place == idx[j : j + 1, :], value, 0.0).astype(BF))
    return jnp.concatenate(parts, axis=1)


def hot_cols(idx_t, lo, count, weight_t=None):
    parts = []
    for j in range(idx_t.shape[1]):
        place = lax.broadcasted_iota(I32, (128, count), 1) + lo
        value = 1.0 if weight_t is None else weight_t[:, j : j + 1]
        parts.append(jnp.where(place == idx_t[:, j : j + 1], value, 0.0).astype(BF))
    return jnp.concatenate(parts, axis=0)


def halo_columns(hidx):
    wide = hidx.astype(F32)
    eye = lax.broadcasted_iota(I32, (32, 32), 0) == lax.broadcasted_iota(I32, (32, 32), 1)
    return [
        jnp.sum(jnp.where(eye, wide[d : d + 1, :], 0.0), axis=1, keepdims=True) for d in range(8)
    ]


def halo_pick(hidx, lo, count):
    place = (lax.broadcasted_iota(I32, (32, count), 1) + lo).astype(F32)
    return jnp.concatenate(
        [jnp.where(place == c, 1.0, 0.0).astype(BF) for c in halo_columns(hidx)], axis=0
    )


def here():
    return lax.axis_index("row"), lax.axis_index("grp")


def shifted(r, g, dr, dg):
    return lax.rem(r + dr + NR, NR), lax.rem(g + dg + NG, NG)


def inside(r, g, dr, dg):
    rr, gg = r + dr, g + dg
    return (rr >= 0) & (rr < NR) & (gg >= 0) & (gg < NG)


def greet(r, g, steps):
    barrier = pltpu.get_barrier_semaphore()
    for dr, dg in steps:
        pl.semaphore_signal(
            barrier, inc=1, device_id=shifted(r, g, dr, dg), device_id_type=MESH
        )
    return lambda: pl.semaphore_wait(barrier, len(steps))


def over(n, fn):
    def step(k, carry):
        fn(k)
        return carry

    lax.fori_loop(1, n, step, 0)


def remote(src, dst, send, recv, place):
    return pltpu.make_async_remote_copy(
        src_ref=src, dst_ref=dst, send_sem=send, recv_sem=recv, device_id=place, device_id_type=MESH
    )


def rows(start, size):
    return pl.ds(pl.multiple_of(start * size, size), size)


GRP_STEPS = [(0, k) for k in range(1, NG)]
ROW_STEPS = [(k, 0) for k in range(1, NR)]
NEAR_STEPS = [(dr, dg) for dr, dg in OFFSETS]
HALO_PEERS = GRP_STEPS + [s for s in NEAR_STEPS if s[0] != 0]
ALL_PEERS = GRP_STEPS + ROW_STEPS + [s for s in NEAR_STEPS if s[0] != 0 and s[1] != 0]


def scatter_grp(r, g, part, land, send, recv, size):
    def copy(k):
        t = lax.rem(g + k, NG)
        return remote(part.at[rows(t, size)], land.at[k - 1], send.at[k - 1], recv.at[k - 1], (r, t))

    return copy


def fetch(pairs, sem):
    copies = [pltpu.make_async_copy(src, dst, sem.at[i]) for i, (src, dst) in enumerate(pairs)]
    for c in copies:
        c.start()

    def wait(*which):
        for i in which:
            copies[i].wait()

    return wait


def halo_kernel(hidx, ct, nf_h, pw_h, gz_h, ein_h, p_out, halo_out, s_out,
                nf, pw, gz, ein, own, land, part, sland, ls, hs, hr, ss, sr):
    r, g = here()
    ready = greet(r, g, HALO_PEERS)
    loaded = fetch([(nf_h, nf), (gz_h, gz), (pw_h, pw), (ein_h, ein)], ls)
    pick = halo_pick(hidx[...], 0, NF)
    loaded(0)
    own[...] = mm(pick, nf[...]).astype(BF)
    ready()
    halo = [
        remote(
            own.at[pl.ds(32 * d, 32)], land.at[pl.ds(32 * d, 32)], hs.at[d], hr.at[d],
            shifted(r, g, dr, dg),
        )
        for d, (dr, dg) in enumerate(OFFSETS)
    ]
    for c in halo:
        c.start()
    loaded(1, 2)
    part[...] = mm(hot_rows(ct[...], 0, GC, pw[...].astype(F32)), gz[...]).astype(BF)
    scat = scatter_grp(r, g, part, sland, ss, sr, NC)
    over(NG, lambda k: scat(k).start())
    loaded(3)
    p_out[0:NF] = mm(nf[...], ein[H : 2 * H]).astype(BF)
    p_out[NX:] = mm(nf[...], ein[2 * H :]).astype(BF)
    for c in halo:
        c.wait()
    for d, (dr, dg) in enumerate(OFFSETS):
        got = land[32 * d : 32 * d + 32]
        halo_out[32 * d : 32 * d + 32] = jnp.where(inside(r, g, -dr, -dg), got, jnp.zeros_like(got))
    p_out[NF:NX] = mm(halo_out[...], ein[H : 2 * H]).astype(BF)
    over(NG, lambda k: scat(k).wait())
    total = part[rows(g, NC)].astype(F32)
    for k in range(NG - 1):
        total += sland[k].astype(F32)
    s_out[...] = total.astype(BF)


def mask_of(count, start, size):
    place = lax.broadcasted_iota(I32, (size, 1), 0) + start
    return jnp.where(place < count, 1.0, 0.0)


def edge_forward_kernel(count, ef, snd, rcv, ptab, ein, ebias, eout, en_out, he_out, ds_out, agg_out,
                        acc):
    step = pl.program_id(0)

    @pl.when(step == 0)
    def _():
        acc[...] = jnp.zeros_like(acc)

    snd_t = jnp.transpose(snd[...])
    rcv_t = jnp.transpose(rcv[...])
    bias = ebias[...].astype(F32)
    per = SUB // 128
    for h in range(BLK // SUB):
        at = slice(h * SUB, (h + 1) * SUB)
        lanes = slice(h * per, (h + 1) * per)
        x = ef[at]
        u = mm(x, ein[0:H]) + bias
        u += mm(hot_cols(snd_t[:, lanes], 0, NX), ptab[0:NX])
        u += mm(hot_cols(rcv_t[:, lanes], 0, NF), ptab[NX:])
        s, slope = silu_parts(u)
        he = s.astype(BF)
        he_out[at] = he
        ds_out[at] = slope.astype(BF)
        m = mask_of(count[0], step * BLK + h * SUB, SUB)
        new = x.astype(F32) + m * mm(he, eout[...])
        en_out[at] = new
        acc[...] += mm(hot_rows(rcv[lanes], 0, NF), (m * new).astype(BF))

    @pl.when(step == pl.num_programs(0) - 1)
    def _():
        agg_out[...] = acc[...].astype(BF)


W_LATE, W_EARLY = 1024, 1536
WROWS = W_LATE + W_EARLY


def lanes_half(p):
    return pl.ds(pl.multiple_of(lax.rem(p, 2) * 128, 128), 128)


class Total:
    def __init__(self, r, g, wbuf, out, base, na, nb, scratch):
        self.r, self.g, self.wbuf, self.out = r, g, wbuf, out
        self.base, self.na, self.nb = base, na, nb
        self.ra, self.rb = na // NG, nb // NR
        self.pa, self.pb = self.ra // 8, self.rb // 4
        (self.a1, self.b1, self.acc_a, self.acc_b, self.a2, self.b2, self.mine_a, self.mine_b,
         self.all_a, self.all_b, *self.sems) = scratch

    @staticmethod
    def scratch(na, nb):
        ra, rb = na // NG, nb // NR
        counts = [NG - 1, NR - 1, NR - 1, NG - 1, NR - 1, NG - 1, NG - 1, NR - 1]
        return [
            pltpu.VMEM((NG - 1, ra, H), BF),
            pltpu.VMEM((NR - 1, rb, H), BF),
            pltpu.VMEM((ra, H), F32),
            pltpu.VMEM((rb, H), F32),
            pltpu.VMEM((NR - 1, ra // 8, 128), F32),
            pltpu.VMEM((NG - 1, rb // 4, 128), F32),
            pltpu.VMEM((ra // 8, 128), F32),
            pltpu.VMEM((rb // 4, 128), F32),
            pltpu.VMEM((ra, H), F32),
            pltpu.VMEM((rb, H), F32),
        ] + [pltpu.SemaphoreType.DMA((n,)) for n in counts for _ in range(2)]

    def block_a(self, t):
        return pl.ds(pl.multiple_of(self.base + t * self.ra, 16), self.ra)

    def block_b(self, t):
        return pl.ds(pl.multiple_of(self.base + self.na + t * self.rb, 16), self.rb)

    def copy(self, stage, src, dst, k, place):
        send, recv = self.sems[2 * stage], self.sems[2 * stage + 1]
        return remote(src, dst, send.at[k - 1], recv.at[k - 1], place)

    def grp(self, k):
        return lax.rem(self.g + k, NG)

    def row(self, k):
        return lax.rem(self.r + k, NR)

    def one_a(self, k):
        t = self.grp(k)
        return self.copy(0, self.wbuf.at[self.block_a(t)], self.a1.at[k - 1], k, (self.r, t))

    def one_b(self, k):
        t = self.row(k)
        return self.copy(1, self.wbuf.at[self.block_b(t)], self.b1.at[k - 1], k, (t, self.g))

    def two_a(self, k):
        t = self.row(k)
        src = self.acc_a.at[rows(t // 2, self.pa), lanes_half(t)]
        return self.copy(2, src, self.a2.at[k - 1], k, (t, self.g))

    def two_b(self, k):
        t = self.grp(k)
        src = self.acc_b.at[rows(t // 2, self.pb), lanes_half(t)]
        return self.copy(3, src, self.b2.at[k - 1], k, (self.r, t))

    def three_a(self, k):
        dst = self.all_a.at[rows(self.r // 2, self.pa), lanes_half(self.r)]
        return self.copy(4, self.mine_a, dst, k, (self.row(k), self.g))

    def three_b(self, k):
        dst = self.all_b.at[rows(self.g // 2, self.pb), lanes_half(self.g)]
        return self.copy(5, self.mine_b, dst, k, (self.r, self.grp(k)))

    def four_a(self, k):
        at = self.out.at[self.block_a(self.g)]
        return self.copy(6, at, at, k, (self.r, self.grp(k)))

    def four_b(self, k):
        at = self.out.at[self.block_b(self.r)]
        return self.copy(7, at, at, k, (self.row(k), self.g))

    def start_one(self):
        over(NR, lambda k: self.one_b(k).start())
        over(NG, lambda k: self.one_a(k).start())

    def start_two(self):
        over(NR, lambda k: self.one_b(k).wait())
        total = self.wbuf[self.block_b(self.r)].astype(F32)
        for k in range(NR - 1):
            total += self.b1[k].astype(F32)
        self.acc_b[...] = total
        over(NG, lambda k: self.two_b(k).start())
        over(NG, lambda k: self.one_a(k).wait())
        total = self.wbuf[self.block_a(self.g)].astype(F32)
        for k in range(NG - 1):
            total += self.a1[k].astype(F32)
        self.acc_a[...] = total
        over(NR, lambda k: self.two_a(k).start())

    def start_three(self):
        over(NG, lambda k: self.two_b(k).wait())
        at = rows(self.g // 2, self.pb), lanes_half(self.g)
        total = self.acc_b[at]
        for k in range(NG - 1):
            total += self.b2[k]
        self.mine_b[...] = total
        self.all_b[at] = total
        over(NG, lambda k: self.three_b(k).start())
        over(NR, lambda k: self.two_a(k).wait())
        at = rows(self.r // 2, self.pa), lanes_half(self.r)
        total = self.acc_a[at]
        for k in range(NR - 1):
            total += self.a2[k]
        self.mine_a[...] = total
        self.all_a[at] = total
        over(NR, lambda k: self.three_a(k).start())

    def start_four(self):
        over(NG, lambda k: self.three_b(k).wait())
        self.out[self.block_b(self.r)] = self.all_b[...].astype(BF)
        over(NR, lambda k: self.four_b(k).start())
        over(NR, lambda k: self.three_a(k).wait())
        self.out[self.block_a(self.g)] = self.all_a[...].astype(BF)
        over(NG, lambda k: self.four_a(k).start())

    def finish(self):
        over(NR, lambda k: self.four_b(k).wait())
        over(NG, lambda k: self.four_a(k).wait())


LATE = (512, 512)
EARLY = (1024, 512)


def rear_kernel(count, nf_h, agg_h, nin_h, nbias_h, nout_h, ct, rw_h, s_h, cin_h, cbias_h, cout_h,
                prol_h, gz_h, ef_h, ge_h, snd, rcv, he_h, ds_h, halo_h, ein_h, eout_h,
                w_out, b_out, q_out, h_out, y_out, dn_out, def_out,
                nf, agg, nin, nbias, nout, rw, s_in, cin, cbias, cout, prol, gz, ef, ge, he, ds, halo,
                ein, eout, ls,
                y, hn, dsn, part, cland, gc_own, gc, q_own, gagg, gyn, ssum, wacc, wbuf, defb, dh, hland,
                bias0, bias1, bl1, bl2,
                css, csr, cgs, cgr, qs, qr, hs, hr, c1s, c1r, c2s, c2r, outs, *sums):
    r, g = here()
    ready = greet(r, g, ALL_PEERS)
    half_way = len(sums) // 2
    early = Total(r, g, wbuf, w_out, W_LATE, *EARLY, sums[:half_way])
    late = Total(r, g, wbuf, w_out, 0, *LATE, sums[half_way:])
    loaded = fetch(
        [(nf_h, nf), (agg_h, agg), (nin_h, nin), (nbias_h, nbias), (nout_h, nout), (rw_h, rw),
         (s_h, s_in), (cin_h, cin), (cbias_h, cbias), (cout_h, cout), (prol_h, prol), (gz_h, gz),
         (eout_h, eout), (ein_h, ein), (halo_h, halo), (ge_h, ge), (ds_h, ds), (ef_h, ef), (he_h, he)],
        ls,
    )

    def grp(k):
        return (r, lax.rem(g + k, NG))

    loaded(0, 1, 2, 3)
    un = mm(nf[...], nin[0:H]) + mm(agg[...], nin[H:]) + nbias[...].astype(F32)
    s, slope = silu_parts(un)
    hn[...] = s.astype(BF)
    dsn[...] = slope.astype(BF)
    loaded(4, 5)
    fresh = nf[...].astype(F32) + mm(hn[...], nout[...])
    y[...] = fresh
    part[...] = mm(hot_rows(ct[...], 0, GC, rw[...].astype(F32)), fresh.astype(BF)).astype(BF)
    ready()
    scat = scatter_grp(r, g, part, cland, css, csr, NC)
    over(NG, lambda k: scat(k).start())
    keep_y = pltpu.make_async_copy(y, y_out, outs.at[0])
    keep_y.start()

    loaded(6, 7, 8, 9, 10)
    sb = s_in[...]
    gcn = mm_nt(sb, prol[...])
    gcnb = gcn.astype(BF)
    gh = mm_nt(gcnb, cout[...])
    over(NG, lambda k: scat(k).wait())
    c = part[rows(g, NC)].astype(F32)
    for k in range(NG - 1):
        c += cland[k].astype(F32)
    cb = c.astype(BF)
    uc = mm(cb, cin[...]) + cbias[...].astype(F32)
    s, slope = silu_parts(uc)
    hc = s.astype(BF)
    guc = gh * slope
    gucb = guc.astype(BF)
    gco = (gcn + mm_nt(gucb, cin[...])).astype(BF)
    gc_own[...] = gco
    gc[rows(g, NC)] = gco

    def give_gc(k):
        return remote(gc_own, gc.at[rows(g, NC)], cgs.at[k - 1], cgr.at[k - 1], grp(k))

    over(NG, lambda k: give_gc(k).start())
    q = (c + mm(hc, cout[...])).astype(BF)
    q_own[...] = q
    q_out[rows(g, NC)] = q

    def give_q(k):
        return remote(q_own, q_out.at[rows(g, NC)], qs.at[k - 1], qr.at[k - 1], grp(k))

    over(NG, lambda k: give_q(k).start())
    wbuf[1792:2048] = mm_tn(cb, gucb).astype(BF)
    wbuf[2048:2304] = mm_tn(hc, gcnb).astype(BF)
    wbuf[2304:2560] = mm_tn(q, sb).astype(BF)
    bias0[...] = jnp.zeros_like(bias0)
    bias0[2:3] = jnp.sum(guc, axis=0, keepdims=True)
    ssum[...] = jnp.zeros_like(ssum)
    wacc[...] = jnp.zeros_like(wacc)
    table = hot_cols(jnp.transpose(ct[...]), 0, GC, jnp.transpose(rw[...].astype(F32)))
    loaded(11)
    over(NG, lambda k: give_gc(k).wait())

    gy = gz[...].astype(F32) + mm(table, gc[...])
    gyb = gy.astype(BF)
    gun = mm_nt(gyb, nout[...]) * dsn[...].astype(F32)
    gunb = gun.astype(BF)
    gagg[...] = mm_nt(gunb, nin[H:]).astype(BF)
    gyn[...] = gy + mm_nt(gunb, nin[0:H])
    wbuf[1024:1280] = mm_tn(nf[...], gunb).astype(BF)
    wbuf[1280:1536] = mm_tn(agg[...], gunb).astype(BF)
    wbuf[1536:1792] = mm_tn(hn[...], gyb).astype(BF)
    bias0[1:2] = jnp.sum(gun, axis=0, keepdims=True)
    early.start_one()

    loaded(12, 13, 14, 15, 16, 17, 18)
    per = SUB // 128

    def keep(step):
        at = pl.ds(pl.multiple_of(step * BLK, BLK), BLK)
        return pltpu.make_async_copy(defb.at[at], def_out.at[at], outs.at[2 + step])

    def edges(step, carry):
        @pl.when(step == 1)
        def _():
            early.start_two()

        @pl.when(step == 2)
        def _():
            early.start_three()

        @pl.when(step == 3)
        def _():
            early.start_four()

        at8 = pl.ds(pl.multiple_of(step * (BLK // 128), BLK // 128), BLK // 128)
        snd8, rcv8 = snd[at8], rcv[at8]
        rcv_t = jnp.transpose(rcv8)
        for h in range(BLK // SUB):
            at = pl.ds(pl.multiple_of(step * BLK + h * SUB, SUB), SUB)
            lanes = slice(h * per, (h + 1) * per)
            m = mask_of(count[0], step * BLK + h * SUB, SUB)
            gen = ge[at].astype(F32) + m * mm(hot_cols(rcv_t[:, lanes], 0, NF), gagg[...])
            gm = (m * gen).astype(BF)
            gue = mm_nt(gm, eout[...]) * ds[at].astype(F32)
            gueb = gue.astype(BF)
            defb[at] = (gen + mm_nt(gueb, ein[0:H])).astype(BF)
            wacc[0:H] += mm_tn(ef[at], gueb)
            wacc[H:] += mm_tn(he[at], gm)
            bias0[0:1] += jnp.sum(gue, axis=0, keepdims=True)
            ssum[0:NX] += mm(hot_rows(snd8[lanes], 0, NX), gueb)
            ssum[NX:] += mm(hot_rows(rcv8[lanes], 0, NF), gueb)
        keep(step).start()
        return carry

    lax.fori_loop(0, EF // BLK, edges, 0)
    sums_b = ssum[...].astype(BF)
    dh[...] = mm_nt(sums_b[NF:NX], ein[H : 2 * H]).astype(BF)
    back = [
        remote(
            dh.at[pl.ds(32 * d, 32)], hland.at[pl.ds(32 * d, 32)], hs.at[d], hr.at[d],
            shifted(r, g, -dr, -dg),
        )
        for d, (dr, dg) in enumerate(OFFSETS)
    ]
    for b in back:
        b.start()

    def one_bias(k):
        return remote(bias0, bl1.at[k - 1], c1s.at[k - 1], c1r.at[k - 1], grp(k))

    def two_bias(k):
        return remote(bias1, bl2.at[k - 1], c2s.at[k - 1], c2r.at[k - 1], (lax.rem(r + k, NR), g))

    over(NG, lambda k: one_bias(k).start())
    wbuf[0:H] = wacc[0:H].astype(BF)
    wbuf[H : 2 * H] = (mm_tn(nf[...], sums_b[0:NF]) + mm_tn(halo[...], sums_b[NF:NX])).astype(BF)
    wbuf[2 * H : 3 * H] = mm_tn(nf[...], sums_b[NX:]).astype(BF)
    wbuf[3 * H : 4 * H] = wacc[H:].astype(BF)
    late.start_one()
    gyn[...] += mm_nt(sums_b[0:NF], ein[H : 2 * H]) + mm_nt(sums_b[NX:], ein[2 * H :])
    keep_dn = pltpu.make_async_copy(gyn, dn_out, outs.at[1])
    keep_dn.start()
    over(NG, lambda k: one_bias(k).wait())
    total = bias0[...]
    for k in range(NG - 1):
        total += bl1[k]
    bias1[...] = total
    over(NR, lambda k: two_bias(k).start())
    early.finish()
    over(NG, lambda k: give_q(k).wait())
    late.start_two()
    for b in back:
        b.wait()
    for d, (dr, dg) in enumerate(OFFSETS):
        got = hland[32 * d : 32 * d + 32]
        h_out[32 * d : 32 * d + 32] = jnp.where(inside(r, g, dr, dg), got, jnp.zeros_like(got))
    late.start_three()
    over(NR, lambda k: two_bias(k).wait())
    total = bias1[...]
    for k in range(NR - 1):
        total += bl2[k]
    b_out[...] = total
    keep_y.wait()
    keep_dn.wait()
    for step in range(EF // BLK):
        keep(step).wait()
    late.start_four()
    late.finish()


PARTS = 4


def result_kernel(b, q, back, dn, y, ct, pw, hidx, prol, de,
                  w_ein, w_eout, w_nin, w_nout, w_cin, w_cout, w_pr,
                  nr_out, dnf_out, def_out, o_eb, o_nb, o_cb,
                  o_ein, o_eout, o_nin, o_nout, o_cin, o_cout, o_pr, qp, pwf):
    step = pl.program_id(0)
    size = NF // PARTS

    @pl.when(step == 0)
    def _():
        qp[...] = mm(q[...], prol[...]).astype(BF)
        pwf[...] = pw[...].astype(F32)
        o_eb[...] = b[0:1]
        o_nb[...] = b[1:2]
        o_cb[...] = b[2:3]

    at = pl.ds(step * (size // 128), size // 128)
    table = hot_rows(ct[at], 0, GC, pwf[at])
    nr_out[...] = y[...] + mm_tn(table, qp[...])
    dnf_out[...] = dn[...] + mm_tn(halo_pick(hidx[...], step * size, size), back[...])
    def_out[...] = de[...].astype(F32)
    for dst, src in ((o_ein, w_ein), (o_eout, w_eout), (o_nin, w_nin), (o_nout, w_nout),
                     (o_cin, w_cin), (o_cout, w_cout), (o_pr, w_pr)):
        dst[...] = src[...].astype(F32)


def body(node_feat, edge_feat, senders, receivers, edge_count, halo_index, coarse_target,
         restrict_weight, prolong_weight, edge_in, edge_bias, edge_out, node_in, node_bias, node_out,
         coarse_in, coarse_bias, coarse_out, prolong, grad_nodes, grad_edges):
    snd = senders.reshape(EF // 128, 128)
    rcv = receivers.reshape(EF // 128, 128)
    ct = coarse_target.reshape(NF // 128, 128)
    rw = restrict_weight.reshape(NF // 128, 128)
    pw = prolong_weight.reshape(NF // 128, 128)
    hidx = halo_index.reshape(8, 32)
    ebias, nbias, cbias = (v.reshape(1, H) for v in (edge_bias, node_bias, coarse_bias))

    def shape(dims, dtype=BF):
        return jax.ShapeDtypeStruct(dims, dtype)

    def sems(*sizes):
        return [pltpu.SemaphoreType.DMA((n,)) for n in sizes]

    def whole(n):
        return [pl.BlockSpec(memory_space=pltpu.VMEM)] * n

    def far(n):
        return [pl.BlockSpec(memory_space=pl.ANY)] * n

    def vmem(*dims, dtype=BF):
        return pltpu.VMEM(dims, dtype)

    smem = pl.BlockSpec(memory_space=pltpu.SMEM)

    def comm(ident, limit):
        return pltpu.CompilerParams(
            collective_id=ident, has_side_effects=True, vmem_limit_bytes=limit * MIB
        )

    ptab, halo, s_own = pl.pallas_call(
        halo_kernel,
        out_shape=[shape((NT, H)), shape((256, H)), shape((NC, H))],
        in_specs=whole(2) + far(4),
        out_specs=whole(3),
        scratch_shapes=[
            vmem(NF, H), vmem(8, 128), vmem(NF, H), vmem(768, H),
            vmem(256, H), vmem(256, H), vmem(GC, H), vmem(NG - 1, NC, H),
        ]
        + sems(4, 8, 8, NG - 1, NG - 1),
        compiler_params=comm(0, LIMIT),
        name="halo",
    )(hidx, ct, node_feat, pw, grad_nodes, edge_in)

    blocks = EF // BLK

    def by_edge(width=H):
        return pl.BlockSpec((BLK, width), lambda i: (i, 0))

    def fixed(dims):
        return pl.BlockSpec(dims, lambda i: (0, 0))

    idx_spec = pl.BlockSpec((BLK // 128, 128), lambda i: (i, 0))
    edge_new, he, ds, agg = pl.pallas_call(
        edge_forward_kernel,
        grid=(blocks,),
        out_shape=[shape((EF, H), F32), shape((EF, H)), shape((EF, H)), shape((NF, H))],
        in_specs=[
            smem, by_edge(), idx_spec, idx_spec, fixed((NT, H)), fixed((768, H)), fixed((1, H)),
            fixed((H, H)),
        ],
        out_specs=[by_edge(), by_edge(), by_edge(), fixed((NF, H))],
        scratch_shapes=[pltpu.VMEM((NF, H), F32)],
        compiler_params=pltpu.CompilerParams(
            dimension_semantics=("arbitrary",), vmem_limit_bytes=LIMIT * MIB
        ),
        name="edge_forward",
    )(edge_count, edge_feat, snd, rcv, ptab, edge_in, ebias, edge_out)

    w_all, b_all, q_all, back, y, dn, de = pl.pallas_call(
        rear_kernel,
        out_shape=[
            shape((WROWS, H)), shape((8, H), F32), shape((GC, H)), shape((256, H)),
            shape((NF, H), F32), shape((NF, H), F32), shape((EF, H)),
        ],
        in_specs=[smem] + far(5) + whole(1) + far(9) + whole(2) + far(5),
        out_specs=whole(4) + far(3),
        scratch_shapes=[
            vmem(NF, H), vmem(NF, H), vmem(512, H), vmem(1, H), vmem(H, H), vmem(8, 128), vmem(NC, H),
            vmem(H, H), vmem(1, H), vmem(H, H), vmem(H, H), vmem(NF, H), vmem(EF, H), vmem(EF, H),
            vmem(EF, H), vmem(EF, H), vmem(256, H), vmem(768, H), vmem(H, H),
        ]
        + sems(19)
        + [
            vmem(NF, H, dtype=F32), vmem(NF, H), vmem(NF, H), vmem(GC, H), vmem(NG - 1, NC, H),
            vmem(NC, H), vmem(GC, H), vmem(NC, H), vmem(NF, H), vmem(NF, H, dtype=F32),
            vmem(NT, H, dtype=F32), vmem(512, H, dtype=F32), vmem(WROWS, H), vmem(EF, H),
            vmem(256, H), vmem(256, H), vmem(8, H, dtype=F32), vmem(8, H, dtype=F32),
            vmem(NG - 1, 8, H, dtype=F32), vmem(NR - 1, 8, H, dtype=F32),
        ]
        + sems(7, 7, 7, 7, 7, 7, 8, 8, 7, 7, 15, 15, 2 + blocks)
        + Total.scratch(*EARLY)
        + Total.scratch(*LATE),
        compiler_params=comm(1, LIMIT),
        name="rear",
    )(edge_count, node_feat, agg, node_in, nbias, node_out, ct, rw, s_own, coarse_in, cbias,
      coarse_out, prolong, grad_nodes, edge_feat, grad_edges, snd, rcv, he, ds, halo, edge_in, edge_out)

    def piece(size, start):
        return pl.BlockSpec((size // PARTS, H), lambda i: (start * PARTS // size + i, 0))

    sizes = (768, 256, 512, 256, 256, 256, 256)
    starts = (0, 768, 1024, 1536, 1792, 2048, 2304)
    (node_result, d_node_feat, d_edge_feat, g_eb, g_nb, g_cb, g_ein, g_eout, g_nin, g_nout, g_cin,
     g_cout, g_pr) = pl.pallas_call(
        result_kernel,
        grid=(PARTS,),
        out_shape=[shape((NF, H), F32), shape((NF, H), F32), shape((EF, H), F32)]
        + [shape((1, H), F32)] * 3
        + [shape((n, H), F32) for n in sizes],
        in_specs=[
            fixed((8, H)), fixed((GC, H)), fixed((256, H)), piece(NF, 0), piece(NF, 0), fixed((8, 128)),
            fixed((8, 128)), fixed((8, 32)), fixed((H, H)), piece(EF, 0),
        ]
        + [piece(n, at) for n, at in zip(sizes, starts)],
        out_specs=[piece(NF, 0), piece(NF, 0), piece(EF, 0)]
        + [fixed((1, H))] * 3
        + [piece(n, 0) for n in sizes],
        scratch_shapes=[vmem(GC, H), vmem(8, 128, dtype=F32)],
        compiler_params=pltpu.CompilerParams(
            dimension_semantics=("arbitrary",), vmem_limit_bytes=LIMIT * MIB
        ),
        name="results",
    )(b_all, q_all, back, dn, y, ct, pw, hidx, prolong, de, *[w_all] * 7)
    return (node_result, edge_new, d_node_feat, d_edge_feat, g_ein, g_eb.reshape(H), g_eout, g_nin,
            g_nb.reshape(H), g_nout, g_cin, g_cb.reshape(H), g_cout, g_pr)


def solution(mesh):
    wide = P(("row", "grp"), None)
    line = P(("row", "grp"))
    in_specs = (
        (wide, wide, line, line, line, P(("row", "grp"), None, None), line, line, line)
        + (P(),) * 10
        + (wide, wide)
    )
    out_specs = (wide,) * 4 + (P(),) * 10
    return jax.shard_map(body, mesh=mesh, in_specs=in_specs, out_specs=out_specs, check_vma=False)
```

```python
import jax
import jax.numpy as jnp
from jax import lax
from jax.experimental import pallas as pl
from jax.experimental.pallas import tpu as pltpu
from jax.sharding import PartitionSpec as P

BF = jnp.bfloat16
F32 = jnp.float32
I32 = jnp.int32
MESH = pl.DeviceIdType.MESH
OFFSETS = ((-1, -1), (-1, 0), (-1, 1), (0, -1), (0, 1), (1, -1), (1, 0), (1, 1))
NR, NG = 16, 8
H = 256
NF = 1024
EF = 4096
NX = 1280
NT = NX + NF
GC = 512
NC = 64
BLK = 1024
SUB = 512
MIB = 1024 * 1024
LIMIT = 60


def mm(a, b):
    return lax.dot_general(a, b, (((1,), (0,)), ((), ())), preferred_element_type=F32)


def mm_nt(a, b):
    return lax.dot_general(a, b, (((1,), (1,)), ((), ())), preferred_element_type=F32)


def mm_tn(a, b):
    return lax.dot_general(a, b, (((0,), (0,)), ((), ())), preferred_element_type=F32)


def silu_parts(u):
    sg = jax.nn.sigmoid(u)
    return u * sg, sg * (1.0 + u * (1.0 - sg))


def hot_rows(idx, lo, count, weight=None):
    parts = []
    for j in range(idx.shape[0]):
        place = lax.broadcasted_iota(I32, (count, 128), 0) + lo
        value = 1.0 if weight is None else weight[j : j + 1, :]
        parts.append(jnp.where(place == idx[j : j + 1, :], value, 0.0).astype(BF))
    return jnp.concatenate(parts, axis=1)


def hot_cols(idx_t, lo, count, weight_t=None):
    parts = []
    for j in range(idx_t.shape[1]):
        place = lax.broadcasted_iota(I32, (128, count), 1) + lo
        value = 1.0 if weight_t is None else weight_t[:, j : j + 1]
        parts.append(jnp.where(place == idx_t[:, j : j + 1], value, 0.0).astype(BF))
    return jnp.concatenate(parts, axis=0)


def halo_columns(hidx):
    wide = hidx.astype(F32)
    eye = lax.broadcasted_iota(I32, (32, 32), 0) == lax.broadcasted_iota(I32, (32, 32), 1)
    return [
        jnp.sum(jnp.where(eye, wide[d : d + 1, :], 0.0), axis=1, keepdims=True) for d in range(8)
    ]


def halo_pick(hidx, lo, count):
    place = (lax.broadcasted_iota(I32, (32, count), 1) + lo).astype(F32)
    return jnp.concatenate(
        [jnp.where(place == c, 1.0, 0.0).astype(BF) for c in halo_columns(hidx)], axis=0
    )


def here():
    return lax.axis_index("row"), lax.axis_index("grp")


def shifted(r, g, dr, dg):
    return lax.rem(r + dr + NR, NR), lax.rem(g + dg + NG, NG)


def inside(r, g, dr, dg):
    rr, gg = r + dr, g + dg
    return (rr >= 0) & (rr < NR) & (gg >= 0) & (gg < NG)


def greet(r, g, steps):
    barrier = pltpu.get_barrier_semaphore()
    for dr, dg in steps:
        pl.semaphore_signal(
            barrier, inc=1, device_id=shifted(r, g, dr, dg), device_id_type=MESH
        )
    return lambda: pl.semaphore_wait(barrier, len(steps))


def over(n, fn):
    def step(k, carry):
        fn(k)
        return carry

    lax.fori_loop(1, n, step, 0)


def remote(src, dst, send, recv, place):
    return pltpu.make_async_remote_copy(
        src_ref=src, dst_ref=dst, send_sem=send, recv_sem=recv, device_id=place, device_id_type=MESH
    )


def rows(start, size):
    return pl.ds(pl.multiple_of(start * size, size), size)


GRP_STEPS = [(0, k) for k in range(1, NG)]
ROW_STEPS = [(k, 0) for k in range(1, NR)]
NEAR_STEPS = [(dr, dg) for dr, dg in OFFSETS]
HALO_PEERS = GRP_STEPS + [s for s in NEAR_STEPS if s[0] != 0]
ALL_PEERS = GRP_STEPS + ROW_STEPS + [s for s in NEAR_STEPS if s[0] != 0 and s[1] != 0]


def scatter_grp(r, g, part, land, send, recv, size):
    def copy(k):
        t = lax.rem(g + k, NG)
        return remote(part.at[rows(t, size)], land.at[k - 1], send.at[k - 1], recv.at[k - 1], (r, t))

    return copy


W_LATE, W_EARLY = 1024, 1536
WROWS = W_LATE + W_EARLY


def lanes_half(p):
    return pl.ds(pl.multiple_of(lax.rem(p, 2) * 128, 128), 128)


class Total:
    def __init__(self, r, g, wbuf, out, base, na, nb, scratch):
        self.r, self.g, self.wbuf, self.out = r, g, wbuf, out
        self.base, self.na, self.nb = base, na, nb
        self.ra, self.rb = na // NG, nb // NR
        self.pa, self.pb = self.ra // 8, self.rb // 4
        (self.a1, self.b1, self.acc_a, self.acc_b, self.a2, self.b2, self.mine_a, self.mine_b,
         self.all_a, self.all_b, *self.sems) = scratch

    @staticmethod
    def scratch(na, nb):
        ra, rb = na // NG, nb // NR
        counts = [NG - 1, NR - 1, NR - 1, NG - 1, NR - 1, NG - 1, NG - 1, NR - 1]
        return [
            pltpu.VMEM((NG - 1, ra, H), BF),
            pltpu.VMEM((NR - 1, rb, H), BF),
            pltpu.VMEM((ra, H), F32),
            pltpu.VMEM((rb, H), F32),
            pltpu.VMEM((NR - 1, ra // 8, 128), F32),
            pltpu.VMEM((NG - 1, rb // 4, 128), F32),
            pltpu.VMEM((ra // 8, 128), F32),
            pltpu.VMEM((rb // 4, 128), F32),
            pltpu.VMEM((ra, H), F32),
            pltpu.VMEM((rb, H), F32),
        ] + [pltpu.SemaphoreType.DMA((n,)) for n in counts for _ in range(2)]

    def block_a(self, t):
        return pl.ds(pl.multiple_of(self.base + t * self.ra, 16), self.ra)

    def block_b(self, t):
        return pl.ds(pl.multiple_of(self.base + self.na + t * self.rb, 16), self.rb)

    def copy(self, stage, src, dst, k, place):
        send, recv = self.sems[2 * stage], self.sems[2 * stage + 1]
        return remote(src, dst, send.at[k - 1], recv.at[k - 1], place)

    def grp(self, k):
        return lax.rem(self.g + k, NG)

    def row(self, k):
        return lax.rem(self.r + k, NR)

    def one_a(self, k):
        t = self.grp(k)
        return self.copy(0, self.wbuf.at[self.block_a(t)], self.a1.at[k - 1], k, (self.r, t))

    def one_b(self, k):
        t = self.row(k)
        return self.copy(1, self.wbuf.at[self.block_b(t)], self.b1.at[k - 1], k, (t, self.g))

    def two_a(self, k):
        t = self.row(k)
        src = self.acc_a.at[rows(t // 2, self.pa), lanes_half(t)]
        return self.copy(2, src, self.a2.at[k - 1], k, (t, self.g))

    def two_b(self, k):
        t = self.grp(k)
        src = self.acc_b.at[rows(t // 2, self.pb), lanes_half(t)]
        return self.copy(3, src, self.b2.at[k - 1], k, (self.r, t))

    def three_a(self, k):
        dst = self.all_a.at[rows(self.r // 2, self.pa), lanes_half(self.r)]
        return self.copy(4, self.mine_a, dst, k, (self.row(k), self.g))

    def three_b(self, k):
        dst = self.all_b.at[rows(self.g // 2, self.pb), lanes_half(self.g)]
        return self.copy(5, self.mine_b, dst, k, (self.r, self.grp(k)))

    def four_a(self, k):
        at = self.out.at[self.block_a(self.g)]
        return self.copy(6, at, at, k, (self.r, self.grp(k)))

    def four_b(self, k):
        at = self.out.at[self.block_b(self.r)]
        return self.copy(7, at, at, k, (self.row(k), self.g))

    def start_one(self):
        over(NR, lambda k: self.one_b(k).start())
        over(NG, lambda k: self.one_a(k).start())

    def start_two(self):
        over(NR, lambda k: self.one_b(k).wait())
        total = self.wbuf[self.block_b(self.r)].astype(F32)
        for k in range(NR - 1):
            total += self.b1[k].astype(F32)
        self.acc_b[...] = total
        over(NG, lambda k: self.two_b(k).start())
        over(NG, lambda k: self.one_a(k).wait())
        total = self.wbuf[self.block_a(self.g)].astype(F32)
        for k in range(NG - 1):
            total += self.a1[k].astype(F32)
        self.acc_a[...] = total
        over(NR, lambda k: self.two_a(k).start())

    def start_three(self):
        over(NG, lambda k: self.two_b(k).wait())
        at = rows(self.g // 2, self.pb), lanes_half(self.g)
        total = self.acc_b[at]
        for k in range(NG - 1):
            total += self.b2[k]
        self.mine_b[...] = total
        self.all_b[at] = total
        over(NG, lambda k: self.three_b(k).start())
        over(NR, lambda k: self.two_a(k).wait())
        at = rows(self.r // 2, self.pa), lanes_half(self.r)
        total = self.acc_a[at]
        for k in range(NR - 1):
            total += self.a2[k]
        self.mine_a[...] = total
        self.all_a[at] = total
        over(NR, lambda k: self.three_a(k).start())

    def start_four(self):
        over(NG, lambda k: self.three_b(k).wait())
        self.out[self.block_b(self.r)] = self.all_b[...].astype(BF)
        over(NR, lambda k: self.four_b(k).start())
        over(NR, lambda k: self.three_a(k).wait())
        self.out[self.block_a(self.g)] = self.all_a[...].astype(BF)
        over(NG, lambda k: self.four_a(k).start())

    def finish(self):
        over(NR, lambda k: self.four_b(k).wait())
        over(NG, lambda k: self.four_a(k).wait())


LATE = (512, 512)
EARLY = (1024, 512)


def mask_of(count, start, size):
    place = lax.broadcasted_iota(I32, (size, 1), 0) + start
    return jnp.where(place < count, 1.0, 0.0)


def fetch(pairs, sem):
    copies = [pltpu.make_async_copy(src, dst, sem.at[i]) for i, (src, dst) in enumerate(pairs)]
    for c in copies:
        c.start()

    def wait(*which):
        for i in which:
            copies[i].wait()

    return wait


def step_kernel(count, hidx, ct, snd, rcv, nf_h, gz_h, pw_h, ein_h, ef_h, ebias_h, eout_h, nin_h,
                nbias_h, nout_h, rw_h, cin_h, cbias_h, cout_h, prol_h, ge_h,
                w_out, b_out, nr_out, dn_out, def_out, en_out,
                nf, gz, pw, ein, ef, ebias, eout, nin, nbias, nout, rw, cin, cbias, cout, prol, ge, ls,
                own, halo, spart, sland, xs, xr, he, ds, enb, acc, agg,
                y, hn, dsn, part, cland, gc_own, gc, q_own, q_all, gagg, gyn, ssum, wacc, wbuf, gueb_s,
                defb, dh, hland, bias0, bias1, bl1, bl2,
                fs, fr, sss, ssr, css, csr, cgs, cgr, qs, qr, hs, hr, c1s, c1r, c2s, c2r, outs, *sums):
    r, g = here()
    ready = greet(r, g, ALL_PEERS)
    half_way = len(sums) // 2
    early = Total(r, g, wbuf, w_out, W_LATE, *EARLY, sums[:half_way])
    late = Total(r, g, wbuf, w_out, 0, *LATE, sums[half_way:])
    loaded = fetch(
        [(nf_h, nf), (gz_h, gz), (pw_h, pw), (ein_h, ein), (ef_h, ef), (ebias_h, ebias), (eout_h, eout),
         (nin_h, nin), (nbias_h, nbias), (nout_h, nout), (rw_h, rw), (cin_h, cin), (cbias_h, cbias),
         (cout_h, cout), (prol_h, prol), (ge_h, ge)],
        ls,
    )
    per = SUB // 128

    def grp(k):
        return (r, lax.rem(g + k, NG))

    def row(k):
        return (lax.rem(r + k, NR), g)

    def bias_of(ref):
        return ref[...].astype(F32).reshape(1, H)

    def swap_halo(src, dst, send, recv, sign):
        return [
            remote(
                src.at[pl.ds(32 * d, 32)], dst.at[pl.ds(32 * d, 32)], send.at[d], recv.at[d],
                shifted(r, g, sign * dr, sign * dg),
            )
            for d, (dr, dg) in enumerate(OFFSETS)
        ]

    def blank_outside(buf, sign):
        for d, (dr, dg) in enumerate(OFFSETS):
            got = buf[32 * d : 32 * d + 32]
            buf[32 * d : 32 * d + 32] = jnp.where(
                inside(r, g, sign * dr, sign * dg), got, jnp.zeros_like(got)
            )

    def by_block(fn):
        def body(step, carry):
            at8 = pl.ds(pl.multiple_of(step * (BLK // 128), BLK // 128), BLK // 128)
            fn(step, at8)
            return carry

        lax.fori_loop(0, EF // BLK, body, 0)

    def sub(step, h):
        at = pl.ds(pl.multiple_of(step * BLK + h * SUB, SUB), SUB)
        return at, slice(h * per, (h + 1) * per), step * BLK + h * SUB

    pick = halo_pick(hidx[...], 0, NF)
    loaded(0)
    own[...] = mm(pick, nf[...]).astype(BF)
    ready()
    there = swap_halo(own, halo, fs, fr, 1)
    for c in there:
        c.start()
    loaded(1, 2)
    spart[...] = mm(hot_rows(ct[...], 0, GC, pw[...].astype(F32)), gz[...]).astype(BF)
    scat_s = scatter_grp(r, g, spart, sland, sss, ssr, NC)
    over(NG, lambda k: scat_s(k).start())

    def gather(step, at8):
        snd_t, rcv_t = jnp.transpose(snd[at8]), jnp.transpose(rcv[at8])
        for h in range(BLK // SUB):
            at, lanes, _ = sub(step, h)
            xs[at] = mm(hot_cols(snd_t[:, lanes], 0, NF), nf[...]).astype(BF)
            xr[at] = mm(hot_cols(rcv_t[:, lanes], 0, NF), nf[...]).astype(BF)

    by_block(gather)
    acc[...] = jnp.zeros_like(acc)
    loaded(3, 4, 5, 6)
    for c in there:
        c.wait()
    blank_outside(halo, -1)

    def keep_en(step):
        at = pl.ds(pl.multiple_of(step * BLK, BLK), BLK)
        return pltpu.make_async_copy(enb.at[at], en_out.at[at], outs.at[step])

    def forward(step, at8):
        snd_t, rcv8 = jnp.transpose(snd[at8]), rcv[at8]
        for h in range(BLK // SUB):
            at, lanes, first = sub(step, h)
            x = ef[at]
            x_s = xs[at] + mm(hot_cols(snd_t[:, lanes], NF, 256), halo[...]).astype(BF)
            xs[at] = x_s
            u = mm(x, ein[0:H]) + mm(x_s, ein[H : 2 * H]) + mm(xr[at], ein[2 * H :]) + bias_of(ebias)
            s, slope = silu_parts(u)
            hidden = s.astype(BF)
            he[at] = hidden
            ds[at] = slope.astype(BF)
            m = mask_of(count[0], first, SUB)
            new = (x.astype(F32) + m * mm(hidden, eout[...])).astype(BF)
            enb[at] = new
            acc[...] += mm(hot_rows(rcv8[lanes], 0, NF), m.astype(BF) * new)
        keep_en(step).start()

    by_block(forward)
    agg[...] = acc[...].astype(BF)

    loaded(7, 8)
    un = mm(nf[...], nin[0:H]) + mm(agg[...], nin[H:]) + bias_of(nbias)
    s, slope = silu_parts(un)
    hn[...] = s.astype(BF)
    dsn[...] = slope.astype(BF)
    loaded(9, 10)
    fresh = nf[...].astype(F32) + mm(hn[...], nout[...])
    y[...] = fresh
    part[...] = mm(hot_rows(ct[...], 0, GC, rw[...].astype(F32)), fresh.astype(BF)).astype(BF)
    scat = scatter_grp(r, g, part, cland, css, csr, NC)
    over(NG, lambda k: scat(k).start())

    loaded(11, 12, 13, 14)
    over(NG, lambda k: scat_s(k).wait())
    total = spart[rows(g, NC)].astype(F32)
    for k in range(NG - 1):
        total += sland[k].astype(F32)
    sb = total.astype(BF)
    gcn = mm_nt(sb, prol[...])
    gcnb = gcn.astype(BF)
    gh = mm_nt(gcnb, cout[...])
    ssum[...] = jnp.zeros_like(ssum)
    wacc[...] = jnp.zeros_like(wacc)
    bias0[...] = jnp.zeros_like(bias0)
    over(NG, lambda k: scat(k).wait())
    c = part[rows(g, NC)].astype(F32)
    for k in range(NG - 1):
        c += cland[k].astype(F32)
    cb = c.astype(BF)
    uc = mm(cb, cin[...]) + bias_of(cbias)
    s, slope = silu_parts(uc)
    hc = s.astype(BF)
    guc = gh * slope
    gucb = guc.astype(BF)
    gco = (gcn + mm_nt(gucb, cin[...])).astype(BF)
    gc_own[...] = gco
    gc[rows(g, NC)] = gco

    def give_gc(k):
        return remote(gc_own, gc.at[rows(g, NC)], cgs.at[k - 1], cgr.at[k - 1], grp(k))

    over(NG, lambda k: give_gc(k).start())
    q = (c + mm(hc, cout[...])).astype(BF)
    q_own[...] = q
    q_all[rows(g, NC)] = q
    wbuf[1792:2048] = mm_tn(cb, gucb).astype(BF)
    wbuf[2048:2304] = mm_tn(hc, gcnb).astype(BF)
    wbuf[2304:2560] = mm_tn(q, sb).astype(BF)
    bias0[2:3] = jnp.sum(guc, axis=0, keepdims=True)
    table = hot_cols(jnp.transpose(ct[...]), 0, GC, jnp.transpose(rw[...].astype(F32)))
    over(NG, lambda k: give_gc(k).wait())

    def give_q(k):
        return remote(q_own, q_all.at[rows(g, NC)], qs.at[k - 1], qr.at[k - 1], grp(k))

    over(NG, lambda k: give_q(k).start())

    gy = gz[...].astype(F32) + mm(table, gc[...])
    gyb = gy.astype(BF)
    gun = mm_nt(gyb, nout[...]) * dsn[...].astype(F32)
    gunb = gun.astype(BF)
    gagg[...] = mm_nt(gunb, nin[H:]).astype(BF)
    gyn[...] = gy + mm_nt(gunb, nin[0:H])
    wbuf[1024:1280] = mm_tn(nf[...], gunb).astype(BF)
    wbuf[1280:1536] = mm_tn(agg[...], gunb).astype(BF)
    wbuf[1536:1792] = mm_tn(hn[...], gyb).astype(BF)
    bias0[1:2] = jnp.sum(gun, axis=0, keepdims=True)
    early.start_one()

    loaded(15)

    def backward(step, at8):
        rcv_t = jnp.transpose(rcv[at8])
        for h in range(BLK // SUB):
            at, lanes, first = sub(step, h)
            m = mask_of(count[0], first, SUB)
            gen = ge[at].astype(F32) + m * mm(hot_cols(rcv_t[:, lanes], 0, NF), gagg[...])
            gm = (m * gen).astype(BF)
            gue = mm_nt(gm, eout[...]) * ds[at].astype(F32)
            gueb = gue.astype(BF)
            gueb_s[at] = gueb
            defb[at] = gen.astype(BF)
            wacc[0:H] += mm_tn(ef[at], gueb)
            wacc[H : 2 * H] += mm_tn(xs[at], gueb)
            wacc[2 * H : 3 * H] += mm_tn(xr[at], gueb)
            wacc[3 * H :] += mm_tn(he[at], gm)
            bias0[0:1] += jnp.sum(gue, axis=0, keepdims=True)

    by_block(backward)
    wbuf[0 : 4 * H] = wacc[...].astype(BF)
    late.start_one()

    def one_bias(k):
        return remote(bias0, bl1.at[k - 1], c1s.at[k - 1], c1r.at[k - 1], grp(k))

    def two_bias(k):
        return remote(bias1, bl2.at[k - 1], c2s.at[k - 1], c2r.at[k - 1], row(k))

    over(NG, lambda k: one_bias(k).start())
    early.start_two()

    def keep_def(step):
        at = pl.ds(pl.multiple_of(step * BLK, BLK), BLK)
        return pltpu.make_async_copy(defb.at[at], def_out.at[at], outs.at[EF // BLK + step])

    def scatter(step, at8):
        snd8, rcv8 = snd[at8], rcv[at8]
        for h in range(BLK // SUB):
            at, lanes, _ = sub(step, h)
            gueb = gueb_s[at]
            ssum[0:NX] += mm(hot_rows(snd8[lanes], 0, NX), gueb)
            ssum[NX:] += mm(hot_rows(rcv8[lanes], 0, NF), gueb)
            defb[at] = (defb[at].astype(F32) + mm_nt(gueb, ein[0:H])).astype(BF)
        keep_def(step).start()

    by_block(scatter)
    sums_b = ssum[...].astype(BF)
    dh[...] = mm_nt(sums_b[NF:NX], ein[H : 2 * H]).astype(BF)
    back = swap_halo(dh, hland, hs, hr, -1)
    for b in back:
        b.start()
    late.start_two()
    early.start_three()
    over(NG, lambda k: one_bias(k).wait())
    total = bias0[...]
    for k in range(NG - 1):
        total += bl1[k]
    bias1[...] = total
    over(NR, lambda k: two_bias(k).start())
    gyn[...] += mm_nt(sums_b[0:NF], ein[H : 2 * H]) + mm_nt(sums_b[NX:], ein[2 * H :])
    late.start_three()
    early.start_four()
    over(NG, lambda k: give_q(k).wait())
    ptable = hot_cols(jnp.transpose(ct[...]), 0, GC, jnp.transpose(pw[...].astype(F32)))
    y[...] += mm(ptable, mm(q_all[...], prol[...]).astype(BF))
    last = 2 * (EF // BLK)
    keep_nr = pltpu.make_async_copy(y, nr_out, outs.at[last])
    keep_nr.start()
    for b in back:
        b.wait()
    blank_outside(hland, 1)
    late.start_four()
    gyn[...] += mm_tn(halo_pick(hidx[...], 0, NF), hland[...])
    keep_dn = pltpu.make_async_copy(gyn, dn_out, outs.at[last + 1])
    keep_dn.start()
    over(NR, lambda k: two_bias(k).wait())
    total = bias1[...]
    for k in range(NR - 1):
        total += bl2[k]
    b_out[...] = total
    early.finish()
    for step in range(EF // BLK):
        keep_en(step).wait()
        keep_def(step).wait()
    keep_nr.wait()
    keep_dn.wait()
    late.finish()


PARTS = 4


def result_kernel(b, nr, dn, de, en, w_ein, w_eout, w_nin, w_nout, w_cin, w_cout, w_pr,
                  o_eb, o_nb, o_cb, nr_out, dnf_out, def_out, en_out,
                  o_ein, o_eout, o_nin, o_nout, o_cin, o_cout, o_pr):
    @pl.when(pl.program_id(0) == 0)
    def _():
        o_eb[...] = b[0:1].reshape(H)
        o_nb[...] = b[1:2].reshape(H)
        o_cb[...] = b[2:3].reshape(H)

    for dst, src in ((nr_out, nr), (dnf_out, dn), (def_out, de), (en_out, en),
                     (o_ein, w_ein), (o_eout, w_eout), (o_nin, w_nin), (o_nout, w_nout),
                     (o_cin, w_cin), (o_cout, w_cout), (o_pr, w_pr)):
        dst[...] = src[...].astype(F32)


def body(node_feat, edge_feat, senders, receivers, edge_count, halo_index, coarse_target,
         restrict_weight, prolong_weight, edge_in, edge_bias, edge_out, node_in, node_bias, node_out,
         coarse_in, coarse_bias, coarse_out, prolong, grad_nodes, grad_edges):
    snd = senders.reshape(EF // 128, 128)
    rcv = receivers.reshape(EF // 128, 128)
    ct = coarse_target.reshape(NF // 128, 128)
    rw = restrict_weight.reshape(NF // 128, 128)
    pw = prolong_weight.reshape(NF // 128, 128)
    hidx = halo_index.reshape(8, 32)

    def shape(dims, dtype=BF):
        return jax.ShapeDtypeStruct(dims, dtype)

    def sems(*sizes):
        return [pltpu.SemaphoreType.DMA((n,)) for n in sizes]

    def whole(n):
        return [pl.BlockSpec(memory_space=pltpu.VMEM)] * n

    def far(n):
        return [pl.BlockSpec(memory_space=pl.ANY)] * n

    def vmem(*dims, dtype=BF):
        return pltpu.VMEM(dims, dtype)

    blocks = EF // BLK
    w_all, b_all, nr, dn, de, en = pl.pallas_call(
        step_kernel,
        out_shape=[
            shape((WROWS, H)), shape((8, H), F32), shape((NF, H), F32), shape((NF, H), F32),
            shape((EF, H)), shape((EF, H)),
        ],
        in_specs=[pl.BlockSpec(memory_space=pltpu.SMEM)] + whole(4) + far(16),
        out_specs=whole(2) + far(4),
        scratch_shapes=[
            vmem(NF, H), vmem(NF, H), vmem(8, 128), vmem(768, H), vmem(EF, H), vmem(H), vmem(H, H),
            vmem(512, H), vmem(H), vmem(H, H), vmem(8, 128), vmem(H, H), vmem(H), vmem(H, H), vmem(H, H),
            vmem(EF, H),
        ]
        + sems(16)
        + [
            vmem(256, H), vmem(256, H), vmem(GC, H), vmem(NG - 1, NC, H), vmem(EF, H), vmem(EF, H),
            vmem(EF, H), vmem(EF, H), vmem(EF, H), vmem(NF, H, dtype=F32), vmem(NF, H),
        ]
        + [
            vmem(NF, H, dtype=F32), vmem(NF, H), vmem(NF, H), vmem(GC, H), vmem(NG - 1, NC, H),
            vmem(NC, H), vmem(GC, H), vmem(NC, H), vmem(GC, H), vmem(NF, H), vmem(NF, H, dtype=F32),
            vmem(NT, H, dtype=F32), vmem(1024, H, dtype=F32), vmem(WROWS, H), vmem(EF, H), vmem(EF, H),
            vmem(256, H), vmem(256, H), vmem(8, H, dtype=F32), vmem(8, H, dtype=F32),
            vmem(NG - 1, 8, H, dtype=F32), vmem(NR - 1, 8, H, dtype=F32),
        ]
        + sems(8, 8, 7, 7, 7, 7, 7, 7, 7, 7, 8, 8, 7, 7, 15, 15, 2 * blocks + 2)
        + Total.scratch(*EARLY)
        + Total.scratch(*LATE),
        compiler_params=pltpu.CompilerParams(
            collective_id=0, has_side_effects=True, vmem_limit_bytes=LIMIT * MIB
        ),
        name="step",
    )(edge_count, hidx, ct, snd, rcv, node_feat, grad_nodes, pw, edge_in, edge_feat, edge_bias, edge_out,
      node_in, node_bias, node_out, rw, coarse_in, coarse_bias, coarse_out, prolong, grad_edges)

    def fixed(*dims):
        return pl.BlockSpec(dims, lambda i: (0,) * len(dims))

    def piece(size, start=0):
        return pl.BlockSpec((size // PARTS, H), lambda i: (start * PARTS // size + i, 0))

    sizes = (768, 256, 512, 256, 256, 256, 256)
    starts = (0, 768, 1024, 1536, 1792, 2048, 2304)
    big = [piece(NF), piece(NF), piece(EF), piece(EF)]
    (g_eb, g_nb, g_cb, node_result, d_node_feat, d_edge_feat, edge_new, g_ein, g_eout, g_nin, g_nout,
     g_cin, g_cout, g_pr) = pl.pallas_call(
        result_kernel,
        grid=(PARTS,),
        out_shape=[shape((H,), F32)] * 3
        + [shape((n, H), F32) for n in (NF, NF, EF, EF) + sizes],
        in_specs=[fixed(8, H)] + big + [piece(n, at) for n, at in zip(sizes, starts)],
        out_specs=[fixed(H)] * 3 + big + [piece(n) for n in sizes],
        compiler_params=pltpu.CompilerParams(
            dimension_semantics=("arbitrary",), vmem_limit_bytes=LIMIT * MIB
        ),
        name="results",
    )(b_all, nr, dn, de, en, *[w_all] * 7)
    return (node_result, edge_new, d_node_feat, d_edge_feat, g_ein, g_eb, g_eout, g_nin, g_nb, g_nout,
            g_cin, g_cb, g_cout, g_pr)


def solution(mesh):
    wide = P(("row", "grp"), None)
    line = P(("row", "grp"))
    in_specs = (
        (wide, wide, line, line, line, P(("row", "grp"), None, None), line, line, line)
        + (P(),) * 10
        + (wide, wide)
    )
    out_specs = (wide,) * 4 + (P(),) * 10
    return jax.shard_map(body, mesh=mesh, in_specs=in_specs, out_specs=out_specs, check_vma=False)
```

```python
import jax
import jax.numpy as jnp
from jax import lax
from jax.experimental import pallas as pl
from jax.experimental.pallas import tpu as pltpu
from jax.sharding import PartitionSpec as P

BF = jnp.bfloat16
F32 = jnp.float32
I32 = jnp.int32
MESH = pl.DeviceIdType.MESH
OFFSETS = ((-1, -1), (-1, 0), (-1, 1), (0, -1), (0, 1), (1, -1), (1, 0), (1, 1))
NR, NG = 16, 8
H = 256
NF = 1024
EF = 4096
NX = 1280
NT = NX + NF
GC = 512
NC = 64
BLK = 1024
SUB = 512
MIB = 1024 * 1024
LIMIT = 60


def mm(a, b):
    return lax.dot_general(a, b, (((1,), (0,)), ((), ())), preferred_element_type=F32)


def mm_nt(a, b):
    return lax.dot_general(a, b, (((1,), (1,)), ((), ())), preferred_element_type=F32)


def mm_tn(a, b):
    return lax.dot_general(a, b, (((0,), (0,)), ((), ())), preferred_element_type=F32)


def silu_parts(u):
    sg = jax.nn.sigmoid(u)
    return u * sg, sg * (1.0 + u * (1.0 - sg))


def hot_rows(idx, lo, count, weight=None):
    parts = []
    for j in range(idx.shape[0]):
        place = lax.broadcasted_iota(I32, (count, 128), 0) + lo
        value = 1.0 if weight is None else weight[j : j + 1, :]
        parts.append(jnp.where(place == idx[j : j + 1, :], value, 0.0).astype(BF))
    return jnp.concatenate(parts, axis=1)


def hot_cols(idx_t, lo, count, weight_t=None):
    parts = []
    for j in range(idx_t.shape[1]):
        place = lax.broadcasted_iota(I32, (128, count), 1) + lo
        value = 1.0 if weight_t is None else weight_t[:, j : j + 1]
        parts.append(jnp.where(place == idx_t[:, j : j + 1], value, 0.0).astype(BF))
    return jnp.concatenate(parts, axis=0)


def halo_columns(hidx):
    wide = hidx.astype(F32)
    eye = lax.broadcasted_iota(I32, (32, 32), 0) == lax.broadcasted_iota(I32, (32, 32), 1)
    return [
        jnp.sum(jnp.where(eye, wide[d : d + 1, :], 0.0), axis=1, keepdims=True) for d in range(8)
    ]


def halo_pick(hidx, lo, count):
    place = (lax.broadcasted_iota(I32, (32, count), 1) + lo).astype(F32)
    return jnp.concatenate(
        [jnp.where(place == c, 1.0, 0.0).astype(BF) for c in halo_columns(hidx)], axis=0
    )


def here():
    return lax.axis_index("row"), lax.axis_index("grp")


def shifted(r, g, dr, dg):
    return lax.rem(r + dr + NR, NR), lax.rem(g + dg + NG, NG)


def inside(r, g, dr, dg):
    rr, gg = r + dr, g + dg
    return (rr >= 0) & (rr < NR) & (gg >= 0) & (gg < NG)


def greet(r, g, steps):
    barrier = pltpu.get_barrier_semaphore()
    for dr, dg in steps:
        pl.semaphore_signal(
            barrier, inc=1, device_id=shifted(r, g, dr, dg), device_id_type=MESH
        )
    return lambda: pl.semaphore_wait(barrier, len(steps))


def over(n, fn):
    def step(k, carry):
        fn(k)
        return carry

    lax.fori_loop(1, n, step, 0)


def remote(src, dst, send, recv, place):
    return pltpu.make_async_remote_copy(
        src_ref=src, dst_ref=dst, send_sem=send, recv_sem=recv, device_id=place, device_id_type=MESH
    )


def both(buf, send, recv, place):
    remote(buf, buf, send, recv, place).wait()


def rows(start, size):
    return pl.ds(pl.multiple_of(start * size, size), size)


GRP_STEPS = [(0, k) for k in range(1, NG)]
ROW_STEPS = [(k, 0) for k in range(1, NR)]
NEAR_STEPS = [(dr, dg) for dr, dg in OFFSETS]
HALO_PEERS = GRP_STEPS + [s for s in NEAR_STEPS if s[0] != 0]
ALL_PEERS = GRP_STEPS + ROW_STEPS + [s for s in NEAR_STEPS if s[0] != 0 and s[1] != 0]


def scatter_grp(r, g, part, land, send, recv, size):
    def copy(k):
        t = lax.rem(g + k, NG)
        return remote(part.at[rows(t, size)], land.at[k - 1], send.at[0], recv.at[0], (r, t))

    return copy


W_LATE, W_EARLY = 1024, 1536
WROWS = W_LATE + W_EARLY


def lanes_half(p):
    return pl.ds(pl.multiple_of(lax.rem(p, 2) * 128, 128), 128)


class Total:
    def __init__(self, r, g, wbuf, out, base, na, nb, scratch):
        self.r, self.g, self.wbuf, self.out = r, g, wbuf, out
        self.base, self.na, self.nb = base, na, nb
        self.ra, self.rb = na // NG, nb // NR
        self.pa, self.pb = self.ra // 8, self.rb // 4
        (self.a1, self.b1, self.acc_a, self.acc_b, self.a2, self.b2, self.mine_a, self.mine_b,
         self.all_a, self.all_b, *self.sems) = scratch

    @staticmethod
    def scratch(na, nb):
        ra, rb = na // NG, nb // NR
        return [
            pltpu.VMEM((NG - 1, ra, H), BF),
            pltpu.VMEM((NR - 1, rb, H), BF),
            pltpu.VMEM((ra, H), F32),
            pltpu.VMEM((rb, H), F32),
            pltpu.VMEM((NR - 1, ra // 8, 128), F32),
            pltpu.VMEM((NG - 1, rb // 4, 128), F32),
            pltpu.VMEM((ra // 8, 128), F32),
            pltpu.VMEM((rb // 4, 128), F32),
            pltpu.VMEM((ra, H), F32),
            pltpu.VMEM((rb, H), F32),
        ] + [pltpu.SemaphoreType.DMA((1,))] * 16

    def block_a(self, t):
        return pl.ds(pl.multiple_of(self.base + t * self.ra, 16), self.ra)

    def block_b(self, t):
        return pl.ds(pl.multiple_of(self.base + self.na + t * self.rb, 16), self.rb)

    def copy(self, stage, src, dst, k, place):
        send, recv = self.sems[2 * stage], self.sems[2 * stage + 1]
        return remote(src, dst, send.at[0], recv.at[0], place)

    def wait(self, stage, buf):
        both(buf, self.sems[2 * stage].at[0], self.sems[2 * stage + 1].at[0], (self.r, self.g))

    def grp(self, k):
        return lax.rem(self.g + k, NG)

    def row(self, k):
        return lax.rem(self.r + k, NR)

    def one_a(self, k):
        t = self.grp(k)
        return self.copy(0, self.wbuf.at[self.block_a(t)], self.a1.at[k - 1], k, (self.r, t))

    def one_b(self, k):
        t = self.row(k)
        return self.copy(1, self.wbuf.at[self.block_b(t)], self.b1.at[k - 1], k, (t, self.g))

    def two_a(self, k):
        t = self.row(k)
        src = self.acc_a.at[rows(t // 2, self.pa), lanes_half(t)]
        return self.copy(2, src, self.a2.at[k - 1], k, (t, self.g))

    def two_b(self, k):
        t = self.grp(k)
        src = self.acc_b.at[rows(t // 2, self.pb), lanes_half(t)]
        return self.copy(3, src, self.b2.at[k - 1], k, (self.r, t))

    def three_a(self, k):
        dst = self.all_a.at[rows(self.r // 2, self.pa), lanes_half(self.r)]
        return self.copy(4, self.mine_a, dst, k, (self.row(k), self.g))

    def three_b(self, k):
        dst = self.all_b.at[rows(self.g // 2, self.pb), lanes_half(self.g)]
        return self.copy(5, self.mine_b, dst, k, (self.r, self.grp(k)))

    def four_a(self, k):
        at = self.out.at[self.block_a(self.g)]
        return self.copy(6, at, at, k, (self.r, self.grp(k)))

    def four_b(self, k):
        at = self.out.at[self.block_b(self.r)]
        return self.copy(7, at, at, k, (self.row(k), self.g))

    def start_one(self):
        over(NR, lambda k: self.one_b(k).start())
        over(NG, lambda k: self.one_a(k).start())

    def start_two(self):
        self.wait(1, self.b1)
        total = self.wbuf[self.block_b(self.r)].astype(F32)
        for k in range(NR - 1):
            total += self.b1[k].astype(F32)
        self.acc_b[...] = total
        over(NG, lambda k: self.two_b(k).start())
        self.wait(0, self.a1)
        total = self.wbuf[self.block_a(self.g)].astype(F32)
        for k in range(NG - 1):
            total += self.a1[k].astype(F32)
        self.acc_a[...] = total
        over(NR, lambda k: self.two_a(k).start())

    def start_three(self):
        self.wait(3, self.b2)
        at = rows(self.g // 2, self.pb), lanes_half(self.g)
        total = self.acc_b[at]
        for k in range(NG - 1):
            total += self.b2[k]
        self.mine_b[...] = total
        self.all_b[at] = total
        over(NG, lambda k: self.three_b(k).start())
        self.wait(2, self.a2)
        at = rows(self.r // 2, self.pa), lanes_half(self.r)
        total = self.acc_a[at]
        for k in range(NR - 1):
            total += self.a2[k]
        self.mine_a[...] = total
        self.all_a[at] = total
        over(NR, lambda k: self.three_a(k).start())

    def start_four(self):
        self.wait(5, self.b2)
        self.out[self.block_b(self.r)] = self.all_b[...].astype(BF)
        over(NR, lambda k: self.four_b(k).start())
        self.wait(4, self.a2)
        self.out[self.block_a(self.g)] = self.all_a[...].astype(BF)
        over(NG, lambda k: self.four_a(k).start())

    def finish(self):
        self.wait(7, self.b1)
        self.wait(6, self.a1)


LATE = (512, 512)
EARLY = (1024, 512)


def mask_of(count, start, size):
    place = lax.broadcasted_iota(I32, (size, 1), 0) + start
    return jnp.where(place < count, 1.0, 0.0)


def fetch(pairs, sem):
    copies = [pltpu.make_async_copy(src, dst, sem.at[i]) for i, (src, dst) in enumerate(pairs)]
    for c in copies:
        c.start()

    def wait(*which):
        for i in which:
            copies[i].wait()

    return wait


def step_kernel(count, hidx, ct, snd, rcv, nf_h, gz_h, pw_h, ein_h, ef_h, ebias_h, eout_h, nin_h,
                nbias_h, nout_h, rw_h, cin_h, cbias_h, cout_h, prol_h, ge_h,
                w_out, b_out, nr_out, dn_out, def_out, en_out,
                nf, gz, pw, ein, ef, ebias, eout, nin, nbias, nout, rw, cin, cbias, cout, prol, ge, ls,
                own, halo, spart, sland, xs, xr, he, ds, enb, acc, agg,
                y, hn, dsn, part, cland, gc_own, gc, q_own, q_all, gagg, gyn, ssum, wacc, wbuf, gueb_s,
                defb, dh, hland, bias0, bias1, bl1, bl2,
                fs, fr, sss, ssr, css, csr, cgs, cgr, qs, qr, hs, hr, c1s, c1r, c2s, c2r, outs, *sums):
    r, g = here()
    ready = greet(r, g, ALL_PEERS)
    half_way = len(sums) // 2
    early = Total(r, g, wbuf, w_out, W_LATE, *EARLY, sums[:half_way])
    late = Total(r, g, wbuf, w_out, 0, *LATE, sums[half_way:])
    loaded = fetch(
        [(nf_h, nf), (gz_h, gz), (pw_h, pw), (ein_h, ein), (ef_h, ef), (ebias_h, ebias), (eout_h, eout),
         (nin_h, nin), (nbias_h, nbias), (nout_h, nout), (rw_h, rw), (cin_h, cin), (cbias_h, cbias),
         (cout_h, cout), (prol_h, prol), (ge_h, ge)],
        ls,
    )
    per = SUB // 128

    def grp(k):
        return (r, lax.rem(g + k, NG))

    def row(k):
        return (lax.rem(r + k, NR), g)

    def bias_of(ref):
        return ref[...].astype(F32).reshape(1, H)

    def swap_halo(src, dst, send, recv, sign):
        return [
            remote(
                src.at[pl.ds(32 * d, 32)], dst.at[pl.ds(32 * d, 32)], send.at[0], recv.at[0],
                shifted(r, g, sign * dr, sign * dg),
            )
            for d, (dr, dg) in enumerate(OFFSETS)
        ]

    def blank_outside(buf, sign):
        for d, (dr, dg) in enumerate(OFFSETS):
            got = buf[32 * d : 32 * d + 32]
            buf[32 * d : 32 * d + 32] = jnp.where(
                inside(r, g, sign * dr, sign * dg), got, jnp.zeros_like(got)
            )

    def by_block(fn):
        def body(step, carry):
            at8 = pl.ds(pl.multiple_of(step * (BLK // 128), BLK // 128), BLK // 128)
            fn(step, at8)
            return carry

        lax.fori_loop(0, EF // BLK, body, 0)

    def sub(step, h):
        at = pl.ds(pl.multiple_of(step * BLK + h * SUB, SUB), SUB)
        return at, slice(h * per, (h + 1) * per), step * BLK + h * SUB

    pick = halo_pick(hidx[...], 0, NF)
    loaded(0)
    own[...] = mm(pick, nf[...]).astype(BF)
    ready()
    there = swap_halo(own, halo, fs, fr, 1)
    for c in there:
        c.start()
    loaded(1, 2)
    spart[...] = mm(hot_rows(ct[...], 0, GC, pw[...].astype(F32)), gz[...]).astype(BF)
    scat_s = scatter_grp(r, g, spart, sland, sss, ssr, NC)
    over(NG, lambda k: scat_s(k).start())

    def gather(step, at8):
        snd_t, rcv_t = jnp.transpose(snd[at8]), jnp.transpose(rcv[at8])
        for h in range(BLK // SUB):
            at, lanes, _ = sub(step, h)
            xs[at] = mm(hot_cols(snd_t[:, lanes], 0, NF), nf[...]).astype(BF)
            xr[at] = mm(hot_cols(rcv_t[:, lanes], 0, NF), nf[...]).astype(BF)

    by_block(gather)
    acc[...] = jnp.zeros_like(acc)
    loaded(3, 4, 5, 6)
    both(halo, fs.at[0], fr.at[0], (r, g))
    blank_outside(halo, -1)

    def keep_en(step):
        at = pl.ds(pl.multiple_of(step * BLK, BLK), BLK)
        return pltpu.make_async_copy(enb.at[at], en_out.at[at], outs.at[step])

    def forward(step, at8):
        snd_t, rcv8 = jnp.transpose(snd[at8]), rcv[at8]
        for h in range(BLK // SUB):
            at, lanes, first = sub(step, h)
            x = ef[at]
            x_s = xs[at] + mm(hot_cols(snd_t[:, lanes], NF, 256), halo[...]).astype(BF)
            xs[at] = x_s
            u = mm(x, ein[0:H]) + mm(x_s, ein[H : 2 * H]) + mm(xr[at], ein[2 * H :]) + bias_of(ebias)
            s, slope = silu_parts(u)
            hidden = s.astype(BF)
            he[at] = hidden
            ds[at] = slope.astype(BF)
            m = mask_of(count[0], first, SUB)
            new = (x.astype(F32) + m * mm(hidden, eout[...])).astype(BF)
            enb[at] = new
            acc[...] += mm(hot_rows(rcv8[lanes], 0, NF), m.astype(BF) * new)
        keep_en(step).start()

    by_block(forward)
    agg[...] = acc[...].astype(BF)

    loaded(7, 8)
    un = mm(nf[...], nin[0:H]) + mm(agg[...], nin[H:]) + bias_of(nbias)
    s, slope = silu_parts(un)
    hn[...] = s.astype(BF)
    dsn[...] = slope.astype(BF)
    loaded(9, 10)
    fresh = nf[...].astype(F32) + mm(hn[...], nout[...])
    y[...] = fresh
    part[...] = mm(hot_rows(ct[...], 0, GC, rw[...].astype(F32)), fresh.astype(BF)).astype(BF)
    scat = scatter_grp(r, g, part, cland, css, csr, NC)
    over(NG, lambda k: scat(k).start())

    loaded(11, 12, 13, 14)
    both(sland, sss.at[0], ssr.at[0], (r, g))
    total = spart[rows(g, NC)].astype(F32)
    for k in range(NG - 1):
        total += sland[k].astype(F32)
    sb = total.astype(BF)
    gcn = mm_nt(sb, prol[...])
    gcnb = gcn.astype(BF)
    gh = mm_nt(gcnb, cout[...])
    ssum[...] = jnp.zeros_like(ssum)
    wacc[...] = jnp.zeros_like(wacc)
    bias0[...] = jnp.zeros_like(bias0)
    both(cland, css.at[0], csr.at[0], (r, g))
    c = part[rows(g, NC)].astype(F32)
    for k in range(NG - 1):
        c += cland[k].astype(F32)
    cb = c.astype(BF)
    uc = mm(cb, cin[...]) + bias_of(cbias)
    s, slope = silu_parts(uc)
    hc = s.astype(BF)
    guc = gh * slope
    gucb = guc.astype(BF)
    gco = (gcn + mm_nt(gucb, cin[...])).astype(BF)
    gc_own[...] = gco
    gc[rows(g, NC)] = gco

    def give_gc(k):
        return remote(gc_own, gc.at[rows(g, NC)], cgs.at[0], cgr.at[0], grp(k))

    over(NG, lambda k: give_gc(k).start())
    q = (c + mm(hc, cout[...])).astype(BF)
    q_own[...] = q
    q_all[rows(g, NC)] = q
    wbuf[1792:2048] = mm_tn(cb, gucb).astype(BF)
    wbuf[2048:2304] = mm_tn(hc, gcnb).astype(BF)
    wbuf[2304:2560] = mm_tn(q, sb).astype(BF)
    bias0[2:3] = jnp.sum(guc, axis=0, keepdims=True)
    table = hot_cols(jnp.transpose(ct[...]), 0, GC, jnp.transpose(rw[...].astype(F32)))
    both(cland, cgs.at[0], cgr.at[0], (r, g))

    def give_q(k):
        return remote(q_own, q_all.at[rows(g, NC)], qs.at[0], qr.at[0], grp(k))

    over(NG, lambda k: give_q(k).start())

    gy = gz[...].astype(F32) + mm(table, gc[...])
    gyb = gy.astype(BF)
    gun = mm_nt(gyb, nout[...]) * dsn[...].astype(F32)
    gunb = gun.astype(BF)
    gagg[...] = mm_nt(gunb, nin[H:]).astype(BF)
    gyn[...] = gy + mm_nt(gunb, nin[0:H])
    wbuf[1024:1280] = mm_tn(nf[...], gunb).astype(BF)
    wbuf[1280:1536] = mm_tn(agg[...], gunb).astype(BF)
    wbuf[1536:1792] = mm_tn(hn[...], gyb).astype(BF)
    bias0[1:2] = jnp.sum(gun, axis=0, keepdims=True)
    early.start_one()

    loaded(15)

    def backward(step, at8):
        rcv_t = jnp.transpose(rcv[at8])
        for h in range(BLK // SUB):
            at, lanes, first = sub(step, h)
            m = mask_of(count[0], first, SUB)
            gen = ge[at].astype(F32) + m * mm(hot_cols(rcv_t[:, lanes], 0, NF), gagg[...])
            gm = (m * gen).astype(BF)
            gue = mm_nt(gm, eout[...]) * ds[at].astype(F32)
            gueb = gue.astype(BF)
            gueb_s[at] = gueb
            defb[at] = gen.astype(BF)
            wacc[0:H] += mm_tn(ef[at], gueb)
            wacc[H : 2 * H] += mm_tn(xs[at], gueb)
            wacc[2 * H : 3 * H] += mm_tn(xr[at], gueb)
            wacc[3 * H :] += mm_tn(he[at], gm)
            bias0[0:1] += jnp.sum(gue, axis=0, keepdims=True)

    by_block(backward)
    wbuf[0 : 4 * H] = wacc[...].astype(BF)
    late.start_one()

    def one_bias(k):
        return remote(bias0, bl1.at[k - 1], c1s.at[0], c1r.at[0], grp(k))

    def two_bias(k):
        return remote(bias1, bl2.at[k - 1], c2s.at[0], c2r.at[0], row(k))

    over(NG, lambda k: one_bias(k).start())
    early.start_two()

    def keep_def(step):
        at = pl.ds(pl.multiple_of(step * BLK, BLK), BLK)
        return pltpu.make_async_copy(defb.at[at], def_out.at[at], outs.at[EF // BLK + step])

    def scatter(step, at8):
        snd8, rcv8 = snd[at8], rcv[at8]
        for h in range(BLK // SUB):
            at, lanes, _ = sub(step, h)
            gueb = gueb_s[at]
            ssum[0:NX] += mm(hot_rows(snd8[lanes], 0, NX), gueb)
            ssum[NX:] += mm(hot_rows(rcv8[lanes], 0, NF), gueb)
            defb[at] = (defb[at].astype(F32) + mm_nt(gueb, ein[0:H])).astype(BF)
        keep_def(step).start()

    by_block(scatter)
    sums_b = ssum[...].astype(BF)
    dh[...] = mm_nt(sums_b[NF:NX], ein[H : 2 * H]).astype(BF)
    back = swap_halo(dh, hland, hs, hr, -1)
    for b in back:
        b.start()
    late.start_two()
    early.start_three()
    both(bl1, c1s.at[0], c1r.at[0], (r, g))
    total = bias0[...]
    for k in range(NG - 1):
        total += bl1[k]
    bias1[...] = total
    over(NR, lambda k: two_bias(k).start())
    gyn[...] += mm_nt(sums_b[0:NF], ein[H : 2 * H]) + mm_nt(sums_b[NX:], ein[2 * H :])
    late.start_three()
    early.start_four()
    both(cland, qs.at[0], qr.at[0], (r, g))
    ptable = hot_cols(jnp.transpose(ct[...]), 0, GC, jnp.transpose(pw[...].astype(F32)))
    y[...] += mm(ptable, mm(q_all[...], prol[...]).astype(BF))
    last = 2 * (EF // BLK)
    keep_nr = pltpu.make_async_copy(y, nr_out, outs.at[last])
    keep_nr.start()
    both(hland, hs.at[0], hr.at[0], (r, g))
    blank_outside(hland, 1)
    late.start_four()
    gyn[...] += mm_tn(halo_pick(hidx[...], 0, NF), hland[...])
    keep_dn = pltpu.make_async_copy(gyn, dn_out, outs.at[last + 1])
    keep_dn.start()
    both(bl2, c2s.at[0], c2r.at[0], (r, g))
    total = bias1[...]
    for k in range(NR - 1):
        total += bl2[k]
    b_out[...] = total
    early.finish()
    for step in range(EF // BLK):
        keep_en(step).wait()
        keep_def(step).wait()
    keep_nr.wait()
    keep_dn.wait()
    late.finish()


SIZES = (768, 256, 512, 256, 256, 256, 256)
CHUNK = 2048


def result_kernel(b, nr_h, dn_h, de_h, en_h, w_h, *refs):
    biases, big, mats = refs[0:3], refs[3:7], refs[7:14]
    nr, dn, de, en, w, wide_de, wide_en, wide_w, in_sem, out_sem = refs[14:]
    chunks = [pl.ds(c * CHUNK, CHUNK) for c in range(EF // CHUNK)]
    arriving, leaving = [], []

    def bring(src, dst):
        arriving.append(pltpu.make_async_copy(src, dst, in_sem.at[len(arriving)]))
        arriving[-1].start()
        return arriving[-1]

    def leave(src, dst):
        leaving.append(pltpu.make_async_copy(src, dst, out_sem.at[len(leaving)]))
        leaving[-1].start()

    edges = []
    for at in chunks:
        for src, mid, wide, dst in ((en_h, en, wide_en, big[0]), (de_h, de, wide_de, big[1])):
            edges.append((bring(src.at[at], mid.at[at]), mid, wide, dst, at))
    nodes = [(bring(src, mid), mid, dst) for src, mid, dst in ((nr_h, nr, big[2]), (dn_h, dn, big[3]))]
    w_here = bring(w_h, w)
    for here_, mid, wide, dst, at in edges:
        here_.wait()
        wide[at] = mid[at].astype(F32)
        leave(wide.at[at], dst.at[at])
    for here_, mid, dst in nodes:
        here_.wait()
        leave(mid, dst)
    w_here.wait()
    first = 0
    for dst, size in zip(mats, SIZES):
        wide_w[first : first + size] = w[first : first + size].astype(F32)
        leave(wide_w.at[pl.ds(first, size)], dst)
        first += size
    for i, dst in enumerate(biases):
        dst[...] = b[i : i + 1].reshape(H)
    for c in leaving:
        c.wait()


def body(node_feat, edge_feat, senders, receivers, edge_count, halo_index, coarse_target,
         restrict_weight, prolong_weight, edge_in, edge_bias, edge_out, node_in, node_bias, node_out,
         coarse_in, coarse_bias, coarse_out, prolong, grad_nodes, grad_edges):
    snd = senders.reshape(EF // 128, 128)
    rcv = receivers.reshape(EF // 128, 128)
    ct = coarse_target.reshape(NF // 128, 128)
    rw = restrict_weight.reshape(NF // 128, 128)
    pw = prolong_weight.reshape(NF // 128, 128)
    hidx = halo_index.reshape(8, 32)

    def shape(dims, dtype=BF):
        return jax.ShapeDtypeStruct(dims, dtype)

    def sems(*sizes):
        return [pltpu.SemaphoreType.DMA((n,)) for n in sizes]

    def whole(n):
        return [pl.BlockSpec(memory_space=pltpu.VMEM)] * n

    def far(n):
        return [pl.BlockSpec(memory_space=pl.ANY)] * n

    def vmem(*dims, dtype=BF):
        return pltpu.VMEM(dims, dtype)

    blocks = EF // BLK
    w_all, b_all, nr, dn, de, en = pl.pallas_call(
        step_kernel,
        out_shape=[
            shape((WROWS, H)), shape((8, H), F32), shape((NF, H), F32), shape((NF, H), F32),
            shape((EF, H)), shape((EF, H)),
        ],
        in_specs=[pl.BlockSpec(memory_space=pltpu.SMEM)] + whole(4) + far(16),
        out_specs=whole(2) + far(4),
        scratch_shapes=[
            vmem(NF, H), vmem(NF, H), vmem(8, 128), vmem(768, H), vmem(EF, H), vmem(H), vmem(H, H),
            vmem(512, H), vmem(H), vmem(H, H), vmem(8, 128), vmem(H, H), vmem(H), vmem(H, H), vmem(H, H),
            vmem(EF, H),
        ]
        + sems(16)
        + [
            vmem(256, H), vmem(256, H), vmem(GC, H), vmem(NG - 1, NC, H), vmem(EF, H), vmem(EF, H),
            vmem(EF, H), vmem(EF, H), vmem(EF, H), vmem(NF, H, dtype=F32), vmem(NF, H),
        ]
        + [
            vmem(NF, H, dtype=F32), vmem(NF, H), vmem(NF, H), vmem(GC, H), vmem(NG - 1, NC, H),
            vmem(NC, H), vmem(GC, H), vmem(NC, H), vmem(GC, H), vmem(NF, H), vmem(NF, H, dtype=F32),
            vmem(NT, H, dtype=F32), vmem(1024, H, dtype=F32), vmem(WROWS, H), vmem(EF, H), vmem(EF, H),
            vmem(256, H), vmem(256, H), vmem(8, H, dtype=F32), vmem(8, H, dtype=F32),
            vmem(NG - 1, 8, H, dtype=F32), vmem(NR - 1, 8, H, dtype=F32),
        ]
        + sems(*[1] * 16, 2 * blocks + 2)
        + Total.scratch(*EARLY)
        + Total.scratch(*LATE),
        compiler_params=pltpu.CompilerParams(
            collective_id=0, has_side_effects=True, vmem_limit_bytes=LIMIT * MIB
        ),
        name="step",
    )(edge_count, hidx, ct, snd, rcv, node_feat, grad_nodes, pw, edge_in, edge_feat, edge_bias, edge_out,
      node_in, node_bias, node_out, rw, coarse_in, coarse_bias, coarse_out, prolong, grad_edges)

    chunks = EF // CHUNK
    g_eb, g_nb, g_cb, edge_new, d_edge_feat, node_result, d_node_feat, *mats = pl.pallas_call(
        result_kernel,
        out_shape=[shape((H,), F32)] * 3 + [shape((n, H), F32) for n in (EF, EF, NF, NF) + SIZES],
        in_specs=whole(1) + far(5),
        out_specs=whole(3) + far(11),
        scratch_shapes=[
            vmem(NF, H, dtype=F32), vmem(NF, H, dtype=F32), vmem(EF, H), vmem(EF, H), vmem(WROWS, H),
            vmem(EF, H, dtype=F32), vmem(EF, H, dtype=F32), vmem(WROWS, H, dtype=F32),
        ]
        + sems(2 * chunks + 3, 2 * chunks + 9),
        compiler_params=pltpu.CompilerParams(vmem_limit_bytes=LIMIT * MIB),
        name="results",
    )(b_all, nr, dn, de, en, w_all)
    g_ein, g_eout, g_nin, g_nout, g_cin, g_cout, g_pr = mats
    return (node_result, edge_new, d_node_feat, d_edge_feat, g_ein, g_eb, g_eout, g_nin, g_nb, g_nout,
            g_cin, g_cb, g_cout, g_pr)


def solution(mesh):
    wide = P(("row", "grp"), None)
    line = P(("row", "grp"))
    in_specs = (
        (wide, wide, line, line, line, P(("row", "grp"), None, None), line, line, line)
        + (P(),) * 10
        + (wide, wide)
    )
    out_specs = (wide,) * 4 + (P(),) * 10
    return jax.shard_map(body, mesh=mesh, in_specs=in_specs, out_specs=out_specs, check_vma=False)
```

```python
import jax
import jax.numpy as jnp
from jax import lax
from jax.experimental import pallas as pl
from jax.experimental.pallas import tpu as pltpu
from jax.sharding import PartitionSpec as P

BF = jnp.bfloat16
F32 = jnp.float32
I32 = jnp.int32
MESH = pl.DeviceIdType.MESH
OFFSETS = ((-1, -1), (-1, 0), (-1, 1), (0, -1), (0, 1), (1, -1), (1, 0), (1, 1))
NR, NG = 16, 8
H = 256
NF = 1024
EF = 4096
NX = 1280
NT = NX + NF
GC = 512
NC = 64
BLK = 2048
SUB = 1024
MIB = 1024 * 1024
LIMIT = 60


def mm(a, b):
    return lax.dot_general(a, b, (((1,), (0,)), ((), ())), preferred_element_type=F32)


def mm_nt(a, b):
    return lax.dot_general(a, b, (((1,), (1,)), ((), ())), preferred_element_type=F32)


def mm_tn(a, b):
    return lax.dot_general(a, b, (((0,), (0,)), ((), ())), preferred_element_type=F32)


def silu_parts(u):
    sg = jax.nn.sigmoid(u)
    return u * sg, sg * (1.0 + u * (1.0 - sg))


def hot_rows(idx, lo, count, weight=None):
    parts = []
    for j in range(idx.shape[0]):
        place = lax.broadcasted_iota(I32, (count, 128), 0) + lo
        value = 1.0 if weight is None else weight[j : j + 1, :]
        parts.append(jnp.where(place == idx[j : j + 1, :], value, 0.0).astype(BF))
    return jnp.concatenate(parts, axis=1)


def hot_cols(idx_t, lo, count, weight_t=None):
    parts = []
    for j in range(idx_t.shape[1]):
        place = lax.broadcasted_iota(I32, (128, count), 1) + lo
        value = 1.0 if weight_t is None else weight_t[:, j : j + 1]
        parts.append(jnp.where(place == idx_t[:, j : j + 1], value, 0.0).astype(BF))
    return jnp.concatenate(parts, axis=0)


def halo_columns(hidx):
    wide = hidx.astype(F32)
    eye = lax.broadcasted_iota(I32, (32, 32), 0) == lax.broadcasted_iota(I32, (32, 32), 1)
    return [
        jnp.sum(jnp.where(eye, wide[d : d + 1, :], 0.0), axis=1, keepdims=True) for d in range(8)
    ]


def halo_pick(hidx, lo, count):
    place = (lax.broadcasted_iota(I32, (32, count), 1) + lo).astype(F32)
    return jnp.concatenate(
        [jnp.where(place == c, 1.0, 0.0).astype(BF) for c in halo_columns(hidx)], axis=0
    )


def here():
    return lax.axis_index("row"), lax.axis_index("grp")


def shifted(r, g, dr, dg):
    return lax.rem(r + dr + NR, NR), lax.rem(g + dg + NG, NG)


def inside(r, g, dr, dg):
    rr, gg = r + dr, g + dg
    return (rr >= 0) & (rr < NR) & (gg >= 0) & (gg < NG)


def greet(r, g, steps):
    barrier = pltpu.get_barrier_semaphore()
    for dr, dg in steps:
        pl.semaphore_signal(
            barrier, inc=1, device_id=shifted(r, g, dr, dg), device_id_type=MESH
        )
    return lambda: pl.semaphore_wait(barrier, len(steps))


def over(n, fn):
    def step(k, carry):
        fn(k)
        return carry

    lax.fori_loop(1, n, step, 0)


def remote(src, dst, send, recv, place):
    return pltpu.make_async_remote_copy(
        src_ref=src, dst_ref=dst, send_sem=send, recv_sem=recv, device_id=place, device_id_type=MESH
    )


def both(buf, send, recv, place):
    remote(buf, buf, send, recv, place).wait()


def rows(start, size):
    return pl.ds(pl.multiple_of(start * size, size), size)


GRP_STEPS = [(0, k) for k in range(1, NG)]
ROW_STEPS = [(k, 0) for k in range(1, NR)]
NEAR_STEPS = [(dr, dg) for dr, dg in OFFSETS]
HALO_PEERS = GRP_STEPS + [s for s in NEAR_STEPS if s[0] != 0]
ALL_PEERS = GRP_STEPS + ROW_STEPS + [s for s in NEAR_STEPS if s[0] != 0 and s[1] != 0]


def scatter_grp(r, g, part, land, send, recv, size):
    def copy(k):
        t = lax.rem(g + k, NG)
        return remote(part.at[rows(t, size)], land.at[k - 1], send.at[0], recv.at[0], (r, t))

    return copy


W_LATE, W_EARLY = 768, 1792
WROWS = W_LATE + W_EARLY


def lanes_half(p):
    return pl.ds(pl.multiple_of(lax.rem(p, 2) * 128, 128), 128)


class Total:
    def __init__(self, r, g, wbuf, out, base, na, nb, scratch):
        self.r, self.g, self.wbuf, self.out = r, g, wbuf, out
        self.base, self.na, self.nb = base, na, nb
        self.ra, self.rb = na // NG, nb // NR
        self.pa = self.ra // 8
        (self.a1, self.b1, self.acc_a, self.mine_b, self.a2, self.b2, self.mine_a, self.all_a,
         *self.sems) = scratch

    @staticmethod
    def scratch(na, nb):
        ra, rb = na // NG, nb // NR
        return [
            pltpu.VMEM((NG - 1, ra, H), BF),
            pltpu.VMEM((NR - 1, rb, H), BF),
            pltpu.VMEM((ra, H), F32),
            pltpu.VMEM((rb, H), BF),
            pltpu.VMEM((NR - 1, ra // 8, 128), F32),
            pltpu.VMEM((NG, rb, H), BF),
            pltpu.VMEM((ra // 8, 128), F32),
            pltpu.VMEM((ra, H), F32),
        ] + [pltpu.SemaphoreType.DMA((1,))] * 14

    def block_a(self, t):
        return pl.ds(pl.multiple_of(self.base + t * self.ra, 16), self.ra)

    def block_b(self, t):
        return pl.ds(pl.multiple_of(self.base + self.na + t * self.rb, 16), self.rb)

    def copy(self, stage, src, dst, place):
        send, recv = self.sems[2 * stage], self.sems[2 * stage + 1]
        return remote(src, dst, send.at[0], recv.at[0], place)

    def wait(self, stage, buf):
        both(buf, self.sems[2 * stage].at[0], self.sems[2 * stage + 1].at[0], (self.r, self.g))

    def grp(self, k):
        return lax.rem(self.g + k, NG)

    def row(self, k):
        return lax.rem(self.r + k, NR)

    def one_a(self, k):
        t = self.grp(k)
        self.copy(0, self.wbuf.at[self.block_a(t)], self.a1.at[k - 1], (self.r, t)).start()

    def one_b(self, k):
        t = self.row(k)
        self.copy(1, self.wbuf.at[self.block_b(t)], self.b1.at[k - 1], (t, self.g)).start()

    def two_a(self, k):
        t = self.row(k)
        src = self.acc_a.at[rows(t // 2, self.pa), lanes_half(t)]
        self.copy(2, src, self.a2.at[k - 1], (t, self.g)).start()

    def two_b(self, k):
        self.copy(3, self.mine_b, self.b2.at[self.g], (self.r, self.grp(k))).start()

    def three_a(self, k):
        dst = self.all_a.at[rows(self.r // 2, self.pa), lanes_half(self.r)]
        self.copy(4, self.mine_a, dst, (self.row(k), self.g)).start()

    def four_a(self, k):
        at = self.out.at[self.block_a(self.g)]
        self.copy(5, at, at, (self.r, self.grp(k))).start()

    def four_b(self, k):
        at = self.out.at[self.block_b(self.r)]
        self.copy(6, at, at, (self.row(k), self.g)).start()

    def start_one(self):
        over(NG, self.one_a)
        over(NR, self.one_b)

    def start_two(self):
        self.wait(1, self.b1)
        total = self.wbuf[self.block_b(self.r)].astype(F32)
        for k in range(NR - 1):
            total += self.b1[k].astype(F32)
        self.mine_b[...] = total.astype(BF)
        self.b2[self.g] = total.astype(BF)
        over(NG, self.two_b)
        self.wait(0, self.a1)
        total = self.wbuf[self.block_a(self.g)].astype(F32)
        for k in range(NG - 1):
            total += self.a1[k].astype(F32)
        self.acc_a[...] = total
        over(NR, self.two_a)

    def start_three(self):
        self.wait(2, self.a2)
        at = rows(self.r // 2, self.pa), lanes_half(self.r)
        total = self.acc_a[at]
        for k in range(NR - 1):
            total += self.a2[k]
        self.mine_a[...] = total
        self.all_a[at] = total
        over(NR, self.three_a)
        self.wait(3, self.b1.at[pl.ds(0, NG - 1)])
        total = self.b2[0].astype(F32)
        for k in range(1, NG):
            total += self.b2[k].astype(F32)
        self.out[self.block_b(self.r)] = total.astype(BF)
        over(NR, self.four_b)

    def start_four(self):
        self.wait(4, self.a2)
        self.out[self.block_a(self.g)] = self.all_a[...].astype(BF)
        over(NG, self.four_a)

    def finish(self):
        self.wait(6, self.b1)
        self.wait(5, self.a1)


LATE = (512, 256)
EARLY = (512, 1280)


def mask_of(count, start, size):
    place = lax.broadcasted_iota(I32, (size, 1), 0) + start
    return jnp.where(place < count, 1.0, 0.0)


def fetch(pairs, sem):
    copies = [pltpu.make_async_copy(src, dst, sem.at[i]) for i, (src, dst) in enumerate(pairs)]
    for c in copies:
        c.start()

    def wait(*which):
        for i in which:
            copies[i].wait()

    return wait


def step_kernel(count, hidx, ct, snd, rcv, nf_h, gz_h, pw_h, ein_h, ef_h, ebias_h, eout_h, nin_h,
                nbias_h, nout_h, rw_h, cin_h, cbias_h, cout_h, prol_h, ge_h,
                w_out, b_out, nr_out, dn_out, def_out, en_out,
                nf, gz, pw, ein, ef, ebias, eout, nin, nbias, nout, rw, cin, cbias, cout, prol, ge, ls,
                own, halo, spart, sland, xs, xr, he, ds, enb, acc, agg,
                y, hn, dsn, part, cland, gc_own, gc, q_own, q_all, gagg, gagg_w, gue0, gyn, ssum, wacc, wbuf, gueb_s,
                defb, dh, hland, bias0, bias1, bl1, bl2,
                fs, fr, sss, ssr, css, csr, cgs, cgr, qs, qr, hs, hr, c1s, c1r, c2s, c2r, outs, *sums):
    r, g = here()
    ready = greet(r, g, ALL_PEERS)
    half_way = len(sums) // 2
    early = Total(r, g, wbuf, w_out, W_LATE, *EARLY, sums[:half_way])
    late = Total(r, g, wbuf, w_out, 0, *LATE, sums[half_way:])
    loaded = fetch(
        [(nf_h, nf), (gz_h, gz), (pw_h, pw), (ein_h, ein), (ef_h, ef), (ebias_h, ebias), (eout_h, eout),
         (nin_h, nin), (nbias_h, nbias), (nout_h, nout), (rw_h, rw), (cin_h, cin), (cbias_h, cbias),
         (cout_h, cout), (prol_h, prol), (ge_h, ge)],
        ls,
    )
    per = SUB // 128

    def grp(k):
        return (r, lax.rem(g + k, NG))

    def row(k):
        return (lax.rem(r + k, NR), g)

    def bias_of(ref):
        return ref[...].astype(F32).reshape(1, H)

    def swap_halo(src, dst, send, recv, sign):
        return [
            remote(
                src.at[pl.ds(32 * d, 32)], dst.at[pl.ds(32 * d, 32)], send.at[0], recv.at[0],
                shifted(r, g, sign * dr, sign * dg),
            )
            for d, (dr, dg) in enumerate(OFFSETS)
        ]

    def blank_outside(buf, sign):
        for d, (dr, dg) in enumerate(OFFSETS):
            got = buf[32 * d : 32 * d + 32]
            buf[32 * d : 32 * d + 32] = jnp.where(
                inside(r, g, sign * dr, sign * dg), got, jnp.zeros_like(got)
            )

    def by_block(fn):
        def body(step, carry):
            at8 = pl.ds(pl.multiple_of(step * (BLK // 128), BLK // 128), BLK // 128)
            fn(step, at8)
            return carry

        lax.fori_loop(0, EF // BLK, body, 0)

    def sub(step, h):
        at = pl.ds(pl.multiple_of(step * BLK + h * SUB, SUB), SUB)
        return at, slice(h * per, (h + 1) * per), step * BLK + h * SUB

    pick = halo_pick(hidx[...], 0, NF)
    loaded(0)
    own[...] = mm(pick, nf[...]).astype(BF)
    ready()
    there = swap_halo(own, halo, fs, fr, 1)
    for c in there:
        c.start()
    loaded(1, 2)
    spart[...] = mm(hot_rows(ct[...], 0, GC, pw[...].astype(F32)), gz[...]).astype(BF)
    scat_s = scatter_grp(r, g, spart, sland, sss, ssr, NC)
    over(NG, lambda k: scat_s(k).start())

    def gather(step, at8):
        snd_t, rcv_t = jnp.transpose(snd[at8]), jnp.transpose(rcv[at8])
        for h in range(BLK // SUB):
            at, lanes, _ = sub(step, h)
            xs[at] = mm(hot_cols(snd_t[:, lanes], 0, NF), nf[...]).astype(BF)
            xr[at] = mm(hot_cols(rcv_t[:, lanes], 0, NF), nf[...]).astype(BF)

    by_block(gather)
    acc[...] = jnp.zeros_like(acc)
    loaded(3, 4, 5, 6)
    both(halo, fs.at[0], fr.at[0], (r, g))
    blank_outside(halo, -1)

    def keep_en(step):
        at = pl.ds(pl.multiple_of(step * BLK, BLK), BLK)
        return pltpu.make_async_copy(enb.at[at], en_out.at[at], outs.at[step])

    def forward(step, at8):
        snd_t, rcv8 = jnp.transpose(snd[at8]), rcv[at8]
        for h in range(BLK // SUB):
            at, lanes, first = sub(step, h)
            x = ef[at]
            x_s = xs[at] + mm(hot_cols(snd_t[:, lanes], NF, 256), halo[...]).astype(BF)
            xs[at] = x_s
            u = mm(x, ein[0:H]) + mm(x_s, ein[H : 2 * H]) + mm(xr[at], ein[2 * H :]) + bias_of(ebias)
            s, slope = silu_parts(u)
            hidden = s.astype(BF)
            he[at] = hidden
            ds[at] = slope.astype(BF)
            m = mask_of(count[0], first, SUB)
            new = (x.astype(F32) + m * mm(hidden, eout[...])).astype(BF)
            enb[at] = new
            acc[...] += mm(hot_rows(rcv8[lanes], 0, NF), m.astype(BF) * new)
        keep_en(step).start()

    by_block(forward)
    agg[...] = acc[...].astype(BF)

    loaded(7, 8)
    un = mm(nf[...], nin[0:H]) + mm(agg[...], nin[H:]) + bias_of(nbias)
    s, slope = silu_parts(un)
    hn[...] = s.astype(BF)
    dsn[...] = slope.astype(BF)
    loaded(9, 10)
    fresh = nf[...].astype(F32) + mm(hn[...], nout[...])
    y[...] = fresh
    part[...] = mm(hot_rows(ct[...], 0, GC, rw[...].astype(F32)), fresh.astype(BF)).astype(BF)
    scat = scatter_grp(r, g, part, cland, css, csr, NC)
    over(NG, lambda k: scat(k).start())

    loaded(11, 12, 13, 14)
    both(sland, sss.at[0], ssr.at[0], (r, g))
    total = spart[rows(g, NC)].astype(F32)
    for k in range(NG - 1):
        total += sland[k].astype(F32)
    sb = total.astype(BF)
    gcn = mm_nt(sb, prol[...])
    gcnb = gcn.astype(BF)
    gh = mm_nt(gcnb, cout[...])
    wacc[...] = jnp.zeros_like(wacc)
    bias0[...] = jnp.zeros_like(bias0)
    loaded(15)

    def given(step, at8):
        for h in range(BLK // SUB):
            at, _, first = sub(step, h)
            mge = (mask_of(count[0], first, SUB) * ge[at].astype(F32)).astype(BF)
            gue0[at] = mm_nt(mge, eout[...])
            wacc[3 * H :] += mm_tn(he[at], mge)

    by_block(given)
    both(cland, css.at[0], csr.at[0], (r, g))
    c = part[rows(g, NC)].astype(F32)
    for k in range(NG - 1):
        c += cland[k].astype(F32)
    cb = c.astype(BF)
    uc = mm(cb, cin[...]) + bias_of(cbias)
    s, slope = silu_parts(uc)
    hc = s.astype(BF)
    guc = gh * slope
    gucb = guc.astype(BF)
    gco = (gcn + mm_nt(gucb, cin[...])).astype(BF)
    gc_own[...] = gco
    gc[rows(g, NC)] = gco

    def give_gc(k):
        return remote(gc_own, gc.at[rows(g, NC)], cgs.at[0], cgr.at[0], grp(k))

    over(NG, lambda k: give_gc(k).start())
    q = (c + mm(hc, cout[...])).astype(BF)
    q_own[...] = q
    q_all[rows(g, NC)] = q
    wbuf[1792:2048] = mm_tn(cb, gucb).astype(BF)
    wbuf[2048:2304] = mm_tn(hc, gcnb).astype(BF)
    wbuf[2304:2560] = mm_tn(q, sb).astype(BF)
    bias0[2:3] = jnp.sum(guc, axis=0, keepdims=True)
    table = hot_cols(jnp.transpose(ct[...]), 0, GC, jnp.transpose(rw[...].astype(F32)))
    acc[...] = jnp.zeros_like(acc)

    def he_sums(step, at8):
        rcv8 = rcv[at8]
        for h in range(BLK // SUB):
            at, lanes, first = sub(step, h)
            mhe = (mask_of(count[0], first, SUB) * he[at].astype(F32)).astype(BF)
            acc[...] += mm(hot_rows(rcv8[lanes], 0, NF), mhe)

    by_block(he_sums)
    ssum[...] = jnp.zeros_like(ssum)
    both(cland, cgs.at[0], cgr.at[0], (r, g))

    def give_q(k):
        return remote(q_own, q_all.at[rows(g, NC)], qs.at[0], qr.at[0], grp(k))

    over(NG, lambda k: give_q(k).start())

    gy = gz[...].astype(F32) + mm(table, gc[...])
    gyb = gy.astype(BF)
    gun = mm_nt(gyb, nout[...]) * dsn[...].astype(F32)
    gunb = gun.astype(BF)
    gagg[...] = mm_nt(gunb, nin[H:]).astype(BF)
    gagg_w[...] = mm_nt(gagg[...], eout[...]).astype(BF)
    wbuf[768:1024] = (wacc[3 * H :] + mm_tn(acc[...].astype(BF), gagg[...])).astype(BF)
    gyn[...] = gy + mm_nt(gunb, nin[0:H])
    wbuf[1024:1280] = mm_tn(nf[...], gunb).astype(BF)
    wbuf[1280:1536] = mm_tn(agg[...], gunb).astype(BF)
    wbuf[1536:1792] = mm_tn(hn[...], gyb).astype(BF)
    bias0[1:2] = jnp.sum(gun, axis=0, keepdims=True)
    early.start_one()


    def backward(step, at8):
        rcv_t = jnp.transpose(rcv[at8])
        for h in range(BLK // SUB):
            at, lanes, first = sub(step, h)
            m = mask_of(count[0], first, SUB)
            gue = (gue0[at] + m * mm(hot_cols(rcv_t[:, lanes], 0, NF), gagg_w[...])) * ds[at].astype(F32)
            gueb = gue.astype(BF)
            gueb_s[at] = gueb
            wacc[0:H] += mm_tn(ef[at], gueb)
            wacc[H : 2 * H] += mm_tn(xs[at], gueb)
            wacc[2 * H : 3 * H] += mm_tn(xr[at], gueb)
            bias0[0:1] += jnp.sum(gue, axis=0, keepdims=True)

    by_block(backward)
    wbuf[0 : 3 * H] = wacc[0 : 3 * H].astype(BF)
    late.start_one()

    def one_bias(k):
        return remote(bias0, bl1.at[g], c1s.at[0], c1r.at[0], grp(k))

    def two_bias(k):
        return remote(bias1, bl2.at[r], c2s.at[0], c2r.at[0], row(k))

    bl1[g] = bias0[...]
    over(NG, lambda k: one_bias(k).start())

    def keep_def(step):
        at = pl.ds(pl.multiple_of(step * BLK, BLK), BLK)
        return pltpu.make_async_copy(defb.at[at], def_out.at[at], outs.at[EF // BLK + step])

    def hooked(hooks, step, h):
        for (at_step, at_h), then in hooks:
            if at_h == h:
                pl.when(step == at_step)(then)

    scatter_hooks = (((0, 1), early.start_two), ((1, 1), late.start_two), ((1, 1), early.start_three))

    def scatter(step, at8):
        snd8, rcv8 = snd[at8], rcv[at8]
        for h in range(BLK // SUB):
            hooked(scatter_hooks, step, h)
            at, lanes, _ = sub(step, h)
            gueb = gueb_s[at]
            ssum[0:NX] += mm(hot_rows(snd8[lanes], 0, NX), gueb)
            ssum[NX:] += mm(hot_rows(rcv8[lanes], 0, NF), gueb)

    widen_hooks = (((0, 1), late.start_three), ((1, 1), early.start_four))

    def edge_grads(step, at8):
        rcv_t = jnp.transpose(rcv[at8])
        for h in range(BLK // SUB):
            hooked(widen_hooks, step, h)
            at, lanes, first = sub(step, h)
            m = mask_of(count[0], first, SUB)
            gen = ge[at].astype(F32) + m * mm(hot_cols(rcv_t[:, lanes], 0, NF), gagg[...])
            defb[at] = (gen + mm_nt(gueb_s[at], ein[0:H])).astype(BF)
        keep_def(step).start()

    by_block(scatter)
    sums_b = ssum[...].astype(BF)
    dh[...] = mm_nt(sums_b[NF:NX], ein[H : 2 * H]).astype(BF)
    back = swap_halo(dh, hland, hs, hr, -1)
    for b in back:
        b.start()
    by_block(edge_grads)
    gyn[...] += mm_nt(sums_b[0:NF], ein[H : 2 * H]) + mm_nt(sums_b[NX:], ein[2 * H :])
    both(cland, qs.at[0], qr.at[0], (r, g))
    ptable = hot_cols(jnp.transpose(ct[...]), 0, GC, jnp.transpose(pw[...].astype(F32)))
    y[...] += mm(ptable, mm(q_all[...], prol[...]).astype(BF))
    last = 2 * (EF // BLK)
    keep_nr = pltpu.make_async_copy(y, nr_out, outs.at[last])
    keep_nr.start()
    late.start_four()
    both(bl1.at[pl.ds(0, NG - 1)], c1s.at[0], c1r.at[0], (r, g))
    total = bl1[0]
    for k in range(1, NG):
        total += bl1[k]
    bias1[...] = total
    bl2[r] = total
    over(NR, lambda k: two_bias(k).start())
    both(hland, hs.at[0], hr.at[0], (r, g))
    blank_outside(hland, 1)
    gyn[...] += mm_tn(halo_pick(hidx[...], 0, NF), hland[...])
    keep_dn = pltpu.make_async_copy(gyn, dn_out, outs.at[last + 1])
    keep_dn.start()
    both(bl2.at[pl.ds(0, NR - 1)], c2s.at[0], c2r.at[0], (r, g))
    total = bl2[0]
    for k in range(1, NR):
        total += bl2[k]
    b_out[...] = total
    early.finish()
    for step in range(EF // BLK):
        keep_en(step).wait()
        keep_def(step).wait()
    keep_nr.wait()
    keep_dn.wait()
    late.finish()


SIZES = (768, 256, 512, 256, 256, 256, 256)
CHUNK = 2048


def result_kernel(b, nr_h, dn_h, de_h, en_h, w_h, *refs):
    biases, big, mats = refs[0:3], refs[3:7], refs[7:14]
    nr, dn, de, en, w, wide_de, wide_en, wide_w, in_sem, out_sem = refs[14:]
    chunks = [pl.ds(c * CHUNK, CHUNK) for c in range(EF // CHUNK)]
    arriving, leaving = [], []

    def bring(src, dst):
        arriving.append(pltpu.make_async_copy(src, dst, in_sem.at[len(arriving)]))
        arriving[-1].start()
        return arriving[-1]

    def leave(src, dst):
        leaving.append(pltpu.make_async_copy(src, dst, out_sem.at[len(leaving)]))
        leaving[-1].start()

    edges = []
    for at in chunks:
        for src, mid, wide, dst in ((en_h, en, wide_en, big[0]), (de_h, de, wide_de, big[1])):
            edges.append((bring(src.at[at], mid.at[at]), mid, wide, dst, at))
    nodes = [(bring(src, mid), mid, dst) for src, mid, dst in ((nr_h, nr, big[2]), (dn_h, dn, big[3]))]
    w_here = bring(w_h, w)
    for here_, mid, wide, dst, at in edges:
        here_.wait()
        wide[at] = mid[at].astype(F32)
        leave(wide.at[at], dst.at[at])
    for here_, mid, dst in nodes:
        here_.wait()
        leave(mid, dst)
    w_here.wait()
    first = 0
    for dst, size in zip(mats, SIZES):
        wide_w[first : first + size] = w[first : first + size].astype(F32)
        leave(wide_w.at[pl.ds(first, size)], dst)
        first += size
    for i, dst in enumerate(biases):
        dst[...] = b[i : i + 1].reshape(H)
    for c in leaving:
        c.wait()


def body(node_feat, edge_feat, senders, receivers, edge_count, halo_index, coarse_target,
         restrict_weight, prolong_weight, edge_in, edge_bias, edge_out, node_in, node_bias, node_out,
         coarse_in, coarse_bias, coarse_out, prolong, grad_nodes, grad_edges):
    snd = senders.reshape(EF // 128, 128)
    rcv = receivers.reshape(EF // 128, 128)
    ct = coarse_target.reshape(NF // 128, 128)
    rw = restrict_weight.reshape(NF // 128, 128)
    pw = prolong_weight.reshape(NF // 128, 128)
    hidx = halo_index.reshape(8, 32)

    def shape(dims, dtype=BF):
        return jax.ShapeDtypeStruct(dims, dtype)

    def sems(*sizes):
        return [pltpu.SemaphoreType.DMA((n,)) for n in sizes]

    def whole(n):
        return [pl.BlockSpec(memory_space=pltpu.VMEM)] * n

    def far(n):
        return [pl.BlockSpec(memory_space=pl.ANY)] * n

    def vmem(*dims, dtype=BF):
        return pltpu.VMEM(dims, dtype)

    blocks = EF // BLK
    w_all, b_all, nr, dn, de, en = pl.pallas_call(
        step_kernel,
        out_shape=[
            shape((WROWS, H)), shape((8, H), F32), shape((NF, H), F32), shape((NF, H), F32),
            shape((EF, H)), shape((EF, H)),
        ],
        in_specs=[pl.BlockSpec(memory_space=pltpu.SMEM)] + whole(4) + far(16),
        out_specs=whole(2) + far(4),
        scratch_shapes=[
            vmem(NF, H), vmem(NF, H), vmem(8, 128), vmem(768, H), vmem(EF, H), vmem(H), vmem(H, H),
            vmem(512, H), vmem(H), vmem(H, H), vmem(8, 128), vmem(H, H), vmem(H), vmem(H, H), vmem(H, H),
            vmem(EF, H),
        ]
        + sems(16)
        + [
            vmem(256, H), vmem(256, H), vmem(GC, H), vmem(NG - 1, NC, H), vmem(EF, H), vmem(EF, H),
            vmem(EF, H), vmem(EF, H), vmem(EF, H), vmem(NF, H, dtype=F32), vmem(NF, H),
        ]
        + [
            vmem(NF, H, dtype=F32), vmem(NF, H), vmem(NF, H), vmem(GC, H), vmem(NG - 1, NC, H),
            vmem(NC, H), vmem(GC, H), vmem(NC, H), vmem(GC, H), vmem(NF, H), vmem(NF, H), vmem(EF, H, dtype=F32), vmem(NF, H, dtype=F32),
            vmem(NT, H, dtype=F32), vmem(1024, H, dtype=F32), vmem(WROWS, H), vmem(EF, H), vmem(EF, H),
            vmem(256, H), vmem(256, H), vmem(8, H, dtype=F32), vmem(8, H, dtype=F32),
            vmem(NG, 8, H, dtype=F32), vmem(NR, 8, H, dtype=F32),
        ]
        + sems(*[1] * 16, 2 * blocks + 2)
        + Total.scratch(*EARLY)
        + Total.scratch(*LATE),
        compiler_params=pltpu.CompilerParams(
            collective_id=0, has_side_effects=True, vmem_limit_bytes=LIMIT * MIB
        ),
        name="step",
    )(edge_count, hidx, ct, snd, rcv, node_feat, grad_nodes, pw, edge_in, edge_feat, edge_bias, edge_out,
      node_in, node_bias, node_out, rw, coarse_in, coarse_bias, coarse_out, prolong, grad_edges)

    chunks = EF // CHUNK
    g_eb, g_nb, g_cb, edge_new, d_edge_feat, node_result, d_node_feat, *mats = pl.pallas_call(
        result_kernel,
        out_shape=[shape((H,), F32)] * 3 + [shape((n, H), F32) for n in (EF, EF, NF, NF) + SIZES],
        in_specs=whole(1) + far(5),
        out_specs=whole(3) + far(11),
        scratch_shapes=[
            vmem(NF, H, dtype=F32), vmem(NF, H, dtype=F32), vmem(EF, H), vmem(EF, H), vmem(WROWS, H),
            vmem(EF, H, dtype=F32), vmem(EF, H, dtype=F32), vmem(WROWS, H, dtype=F32),
        ]
        + sems(2 * chunks + 3, 2 * chunks + 9),
        compiler_params=pltpu.CompilerParams(vmem_limit_bytes=LIMIT * MIB),
        name="results",
    )(b_all, nr, dn, de, en, w_all)
    g_ein, g_eout, g_nin, g_nout, g_cin, g_cout, g_pr = mats
    return (node_result, edge_new, d_node_feat, d_edge_feat, g_ein, g_eb, g_eout, g_nin, g_nb, g_nout,
            g_cin, g_cb, g_cout, g_pr)


def solution(mesh):
    wide = P(("row", "grp"), None)
    line = P(("row", "grp"))
    in_specs = (
        (wide, wide, line, line, line, P(("row", "grp"), None, None), line, line, line)
        + (P(),) * 10
        + (wide, wide)
    )
    out_specs = (wide,) * 4 + (P(),) * 10
    return jax.shard_map(body, mesh=mesh, in_specs=in_specs, out_specs=out_specs, check_vma=False)
```

```python
import jax
import jax.numpy as jnp
from jax import lax
from jax.experimental import pallas as pl
from jax.experimental.pallas import tpu as pltpu
from jax.sharding import PartitionSpec as P

BF = jnp.bfloat16
F32 = jnp.float32
I32 = jnp.int32
MESH = pl.DeviceIdType.MESH
OFFSETS = ((-1, -1), (-1, 0), (-1, 1), (0, -1), (0, 1), (1, -1), (1, 0), (1, 1))
NR, NG = 16, 8
H = 256
NF = 1024
EF = 4096
NX = 1280
NT = NX + NF
GC = 512
NC = 64
BLK = 2048
SUB = 1024
MIB = 1024 * 1024
LIMIT = 60


def mm(a, b):
    return lax.dot_general(a, b, (((1,), (0,)), ((), ())), preferred_element_type=F32)


def mm_nt(a, b):
    return lax.dot_general(a, b, (((1,), (1,)), ((), ())), preferred_element_type=F32)


def mm_tn(a, b):
    return lax.dot_general(a, b, (((0,), (0,)), ((), ())), preferred_element_type=F32)


def silu_parts(u):
    sg = jax.nn.sigmoid(u)
    return u * sg, sg * (1.0 + u * (1.0 - sg))


def hot_rows(idx, lo, count, weight=None):
    parts = []
    for j in range(idx.shape[0]):
        place = lax.broadcasted_iota(I32, (count, 128), 0) + lo
        value = 1.0 if weight is None else weight[j : j + 1, :]
        parts.append(jnp.where(place == idx[j : j + 1, :], value, 0.0).astype(BF))
    return jnp.concatenate(parts, axis=1)


def hot_cols(idx_t, lo, count, weight_t=None):
    parts = []
    for j in range(idx_t.shape[1]):
        place = lax.broadcasted_iota(I32, (128, count), 1) + lo
        value = 1.0 if weight_t is None else weight_t[:, j : j + 1]
        parts.append(jnp.where(place == idx_t[:, j : j + 1], value, 0.0).astype(BF))
    return jnp.concatenate(parts, axis=0)


def halo_columns(hidx):
    wide = hidx.astype(F32)
    eye = lax.broadcasted_iota(I32, (32, 32), 0) == lax.broadcasted_iota(I32, (32, 32), 1)
    return [
        jnp.sum(jnp.where(eye, wide[d : d + 1, :], 0.0), axis=1, keepdims=True) for d in range(8)
    ]


def halo_pick(hidx, lo, count):
    place = (lax.broadcasted_iota(I32, (32, count), 1) + lo).astype(F32)
    return jnp.concatenate(
        [jnp.where(place == c, 1.0, 0.0).astype(BF) for c in halo_columns(hidx)], axis=0
    )


def here():
    return lax.axis_index("row"), lax.axis_index("grp")


def shifted(r, g, dr, dg):
    return lax.rem(r + dr + NR, NR), lax.rem(g + dg + NG, NG)


def inside(r, g, dr, dg):
    rr, gg = r + dr, g + dg
    return (rr >= 0) & (rr < NR) & (gg >= 0) & (gg < NG)


def greet(r, g, steps):
    barrier = pltpu.get_barrier_semaphore()
    for dr, dg in steps:
        pl.semaphore_signal(
            barrier, inc=1, device_id=shifted(r, g, dr, dg), device_id_type=MESH
        )
    return lambda: pl.semaphore_wait(barrier, len(steps))


def over(n, fn):
    def step(k, carry):
        fn(k)
        return carry

    lax.fori_loop(1, n, step, 0)


def remote(src, dst, send, recv, place):
    return pltpu.make_async_remote_copy(
        src_ref=src, dst_ref=dst, send_sem=send, recv_sem=recv, device_id=place, device_id_type=MESH
    )


def both(buf, send, recv, place):
    remote(buf, buf, send, recv, place).wait()


def rows(start, size):
    return pl.ds(pl.multiple_of(start * size, size), size)


GRP_STEPS = [(0, k) for k in range(1, NG)]
ROW_STEPS = [(k, 0) for k in range(1, NR)]
NEAR_STEPS = [(dr, dg) for dr, dg in OFFSETS]
HALO_PEERS = GRP_STEPS + [s for s in NEAR_STEPS if s[0] != 0]
ALL_PEERS = GRP_STEPS + ROW_STEPS + [s for s in NEAR_STEPS if s[0] != 0 and s[1] != 0]


def scatter_grp(r, g, part, land, send, recv, size):
    def copy(k):
        t = lax.rem(g + k, NG)
        return remote(part.at[rows(t, size)], land.at[k - 1], send.at[0], recv.at[0], (r, t))

    return copy


W_LATE, W_EARLY = 768, 1792
WROWS = W_LATE + W_EARLY


def lanes_half(p):
    return pl.ds(pl.multiple_of(lax.rem(p, 2) * 128, 128), 128)


class Total:
    def __init__(self, r, g, wbuf, out, base, na, nb, scratch):
        self.r, self.g, self.wbuf, self.out = r, g, wbuf, out
        self.base, self.na, self.nb = base, na, nb
        self.ra, self.rb = na // NG, nb // NR
        self.pa = self.ra // 8
        (self.a1, self.b1, self.acc_a, self.mine_b, self.a2, self.b2, self.mine_a, self.all_a,
         *self.sems) = scratch

    @staticmethod
    def scratch(na, nb):
        ra, rb = na // NG, nb // NR
        return [
            pltpu.VMEM((NG - 1, ra, H), BF),
            pltpu.VMEM((NR - 1, rb, H), BF),
            pltpu.VMEM((ra, H), F32),
            pltpu.VMEM((rb, H), BF),
            pltpu.VMEM((NR - 1, ra // 8, 128), F32),
            pltpu.VMEM((NG, rb, H), BF),
            pltpu.VMEM((ra // 8, 128), F32),
            pltpu.VMEM((ra, H), F32),
        ] + [pltpu.SemaphoreType.DMA((1,))] * 14

    def block_a(self, t):
        return pl.ds(pl.multiple_of(self.base + t * self.ra, 16), self.ra)

    def block_b(self, t):
        return pl.ds(pl.multiple_of(self.base + self.na + t * self.rb, 16), self.rb)

    def copy(self, stage, src, dst, place):
        send, recv = self.sems[2 * stage], self.sems[2 * stage + 1]
        return remote(src, dst, send.at[0], recv.at[0], place)

    def wait(self, stage, buf):
        both(buf, self.sems[2 * stage].at[0], self.sems[2 * stage + 1].at[0], (self.r, self.g))

    def grp(self, k):
        return lax.rem(self.g + k, NG)

    def row(self, k):
        return lax.rem(self.r + k, NR)

    def one_a(self, k):
        t = self.grp(k)
        self.copy(0, self.wbuf.at[self.block_a(t)], self.a1.at[k - 1], (self.r, t)).start()

    def one_b(self, k):
        t = self.row(k)
        self.copy(1, self.wbuf.at[self.block_b(t)], self.b1.at[k - 1], (t, self.g)).start()

    def two_a(self, k):
        t = self.row(k)
        src = self.acc_a.at[rows(t // 2, self.pa), lanes_half(t)]
        self.copy(2, src, self.a2.at[k - 1], (t, self.g)).start()

    def two_b(self, k):
        self.copy(3, self.mine_b, self.b2.at[self.g], (self.r, self.grp(k))).start()

    def three_a(self, k):
        dst = self.all_a.at[rows(self.r // 2, self.pa), lanes_half(self.r)]
        self.copy(4, self.mine_a, dst, (self.row(k), self.g)).start()

    def four_a(self, k):
        at = self.out.at[self.block_a(self.g)]
        self.copy(5, at, at, (self.r, self.grp(k))).start()

    def four_b(self, k):
        at = self.out.at[self.block_b(self.r)]
        self.copy(6, at, at, (self.row(k), self.g)).start()

    def start_one(self):
        over(NG, self.one_a)
        over(NR, self.one_b)

    def start_two(self):
        self.wait(1, self.b1)
        total = self.wbuf[self.block_b(self.r)].astype(F32)
        for k in range(NR - 1):
            total += self.b1[k].astype(F32)
        self.mine_b[...] = total.astype(BF)
        self.b2[self.g] = total.astype(BF)
        over(NG, self.two_b)
        self.wait(0, self.a1)
        total = self.wbuf[self.block_a(self.g)].astype(F32)
        for k in range(NG - 1):
            total += self.a1[k].astype(F32)
        self.acc_a[...] = total
        over(NR, self.two_a)

    def start_three(self):
        self.wait(2, self.a2)
        at = rows(self.r // 2, self.pa), lanes_half(self.r)
        total = self.acc_a[at]
        for k in range(NR - 1):
            total += self.a2[k]
        self.mine_a[...] = total
        self.all_a[at] = total
        over(NR, self.three_a)
        self.wait(3, self.b1.at[pl.ds(0, NG - 1)])
        total = self.b2[0].astype(F32)
        for k in range(1, NG):
            total += self.b2[k].astype(F32)
        self.out[self.block_b(self.r)] = total.astype(BF)
        over(NR, self.four_b)

    def start_four(self):
        self.wait(4, self.a2)
        self.out[self.block_a(self.g)] = self.all_a[...].astype(BF)
        over(NG, self.four_a)

    def finish(self):
        self.wait(6, self.b1)
        self.wait(5, self.a1)


LATE = (512, 256)
EARLY = (512, 1280)


def mask_of(count, start, size):
    place = lax.broadcasted_iota(I32, (size, 1), 0) + start
    return jnp.where(place < count, 1.0, 0.0)


def fetch(pairs, sem):
    copies = [pltpu.make_async_copy(src, dst, sem.at[i]) for i, (src, dst) in enumerate(pairs)]
    for c in copies:
        c.start()

    def wait(*which):
        for i in which:
            copies[i].wait()

    return wait


def step_kernel(count, hidx_h, ct_h, snd_h, rcv_h, nf_h, gz_h, pw_h, ein_h, ef_h, ebias_h, eout_h, nin_h,
                nbias_h, nout_h, rw_h, cin_h, cbias_h, cout_h, prol_h, ge_h,
                w_hbm, b_hbm, nr_out, dn_out, def_out, en_out,
                hidx, ct, snd, rcv, small, w_out, b_out,
                nf, gz, pw, ein, ef, ebias, eout, nin, nbias, nout, rw, cin, cbias, cout, prol, ge, ls,
                own, halo, spart, sland, xs, xr, he, ds, enb, acc, agg,
                y, hn, dsn, part, cland, gc_own, gc, q_own, q_all, gagg, gagg_w, gue0, gyn, ssum, wacc, wbuf, gueb_s,
                defb, dh, hland, bias0, bias1, bl1, bl2,
                fs, fr, sss, ssr, css, csr, cgs, cgr, qs, qr, hs, hr, c1s, c1r, c2s, c2r, outs, *sums):
    r, g = here()
    half_way = len(sums) // 2
    early = Total(r, g, wbuf, w_out, W_LATE, *EARLY, sums[:half_way])
    late = Total(r, g, wbuf, w_out, 0, *LATE, sums[half_way:])
    indexed = fetch([(hidx_h, hidx), (ct_h, ct), (snd_h, snd), (rcv_h, rcv)], small)
    loaded = fetch(
        [(nf_h, nf), (gz_h, gz), (pw_h, pw), (ein_h, ein), (ef_h, ef), (ebias_h, ebias), (eout_h, eout),
         (nin_h, nin), (nbias_h, nbias), (nout_h, nout), (rw_h, rw), (cin_h, cin), (cbias_h, cbias),
         (cout_h, cout), (prol_h, prol), (ge_h, ge)],
        ls,
    )
    ready = greet(r, g, ALL_PEERS)
    per = SUB // 128

    def grp(k):
        return (r, lax.rem(g + k, NG))

    def row(k):
        return (lax.rem(r + k, NR), g)

    def bias_of(ref):
        return ref[...].astype(F32).reshape(1, H)

    def swap_halo(src, dst, send, recv, sign):
        return [
            remote(
                src.at[pl.ds(32 * d, 32)], dst.at[pl.ds(32 * d, 32)], send.at[0], recv.at[0],
                shifted(r, g, sign * dr, sign * dg),
            )
            for d, (dr, dg) in enumerate(OFFSETS)
        ]

    def blank_outside(buf, sign):
        for d, (dr, dg) in enumerate(OFFSETS):
            got = buf[32 * d : 32 * d + 32]
            buf[32 * d : 32 * d + 32] = jnp.where(
                inside(r, g, sign * dr, sign * dg), got, jnp.zeros_like(got)
            )

    def by_block(fn):
        def body(step, carry):
            at8 = pl.ds(pl.multiple_of(step * (BLK // 128), BLK // 128), BLK // 128)
            fn(step, at8)
            return carry

        lax.fori_loop(0, EF // BLK, body, 0)

    def sub(step, h):
        at = pl.ds(pl.multiple_of(step * BLK + h * SUB, SUB), SUB)
        return at, slice(h * per, (h + 1) * per), step * BLK + h * SUB

    indexed(0)
    pick = halo_pick(hidx[...], 0, NF)
    loaded(0)
    own[...] = mm(pick, nf[...]).astype(BF)
    ready()
    there = swap_halo(own, halo, fs, fr, 1)
    for c in there:
        c.start()
    indexed(1, 2, 3)
    loaded(1, 2)
    spart[...] = mm(hot_rows(ct[...], 0, GC, pw[...].astype(F32)), gz[...]).astype(BF)
    scat_s = scatter_grp(r, g, spart, sland, sss, ssr, NC)
    over(NG, lambda k: scat_s(k).start())

    def gather(step, at8):
        snd_t, rcv_t = jnp.transpose(snd[at8]), jnp.transpose(rcv[at8])
        for h in range(BLK // SUB):
            at, lanes, _ = sub(step, h)
            xs[at] = mm(hot_cols(snd_t[:, lanes], 0, NF), nf[...]).astype(BF)
            xr[at] = mm(hot_cols(rcv_t[:, lanes], 0, NF), nf[...]).astype(BF)

    by_block(gather)
    acc[...] = jnp.zeros_like(acc)
    loaded(3, 4, 5, 6)
    both(halo, fs.at[0], fr.at[0], (r, g))
    blank_outside(halo, -1)

    def keep_en(step):
        at = pl.ds(pl.multiple_of(step * BLK, BLK), BLK)
        return pltpu.make_async_copy(enb.at[at], en_out.at[at], outs.at[step])

    def forward(step, at8):
        snd_t, rcv8 = jnp.transpose(snd[at8]), rcv[at8]
        for h in range(BLK // SUB):
            at, lanes, first = sub(step, h)
            x = ef[at]
            x_s = xs[at] + mm(hot_cols(snd_t[:, lanes], NF, 256), halo[...]).astype(BF)
            xs[at] = x_s
            u = mm(x, ein[0:H]) + mm(x_s, ein[H : 2 * H]) + mm(xr[at], ein[2 * H :]) + bias_of(ebias)
            s, slope = silu_parts(u)
            hidden = s.astype(BF)
            he[at] = hidden
            ds[at] = slope.astype(BF)
            m = mask_of(count[0], first, SUB)
            new = (x.astype(F32) + m * mm(hidden, eout[...])).astype(BF)
            enb[at] = new
            acc[...] += mm(hot_rows(rcv8[lanes], 0, NF), m.astype(BF) * new)
        keep_en(step).start()

    by_block(forward)
    agg[...] = acc[...].astype(BF)

    loaded(7, 8)
    un = mm(nf[...], nin[0:H]) + mm(agg[...], nin[H:]) + bias_of(nbias)
    s, slope = silu_parts(un)
    hn[...] = s.astype(BF)
    dsn[...] = slope.astype(BF)
    loaded(9, 10)
    fresh = nf[...].astype(F32) + mm(hn[...], nout[...])
    y[...] = fresh
    part[...] = mm(hot_rows(ct[...], 0, GC, rw[...].astype(F32)), fresh.astype(BF)).astype(BF)
    scat = scatter_grp(r, g, part, cland, css, csr, NC)
    over(NG, lambda k: scat(k).start())

    loaded(11, 12, 13, 14)
    both(sland, sss.at[0], ssr.at[0], (r, g))
    total = spart[rows(g, NC)].astype(F32)
    for k in range(NG - 1):
        total += sland[k].astype(F32)
    sb = total.astype(BF)
    gcn = mm_nt(sb, prol[...])
    gcnb = gcn.astype(BF)
    gh = mm_nt(gcnb, cout[...])
    wacc[...] = jnp.zeros_like(wacc)
    bias0[...] = jnp.zeros_like(bias0)
    loaded(15)

    def given(step, at8):
        for h in range(BLK // SUB):
            at, _, first = sub(step, h)
            mge = (mask_of(count[0], first, SUB) * ge[at].astype(F32)).astype(BF)
            gue0[at] = mm_nt(mge, eout[...])
            wacc[3 * H :] += mm_tn(he[at], mge)

    by_block(given)
    both(cland, css.at[0], csr.at[0], (r, g))
    c = part[rows(g, NC)].astype(F32)
    for k in range(NG - 1):
        c += cland[k].astype(F32)
    cb = c.astype(BF)
    uc = mm(cb, cin[...]) + bias_of(cbias)
    s, slope = silu_parts(uc)
    hc = s.astype(BF)
    guc = gh * slope
    gucb = guc.astype(BF)
    gco = (gcn + mm_nt(gucb, cin[...])).astype(BF)
    gc_own[...] = gco
    gc[rows(g, NC)] = gco

    def give_gc(k):
        return remote(gc_own, gc.at[rows(g, NC)], cgs.at[0], cgr.at[0], grp(k))

    over(NG, lambda k: give_gc(k).start())
    q = (c + mm(hc, cout[...])).astype(BF)
    q_own[...] = q
    q_all[rows(g, NC)] = q
    wbuf[1792:2048] = mm_tn(cb, gucb).astype(BF)
    wbuf[2048:2304] = mm_tn(hc, gcnb).astype(BF)
    wbuf[2304:2560] = mm_tn(q, sb).astype(BF)
    bias0[2:3] = jnp.sum(guc, axis=0, keepdims=True)
    table = hot_cols(jnp.transpose(ct[...]), 0, GC, jnp.transpose(rw[...].astype(F32)))
    acc[...] = jnp.zeros_like(acc)

    def he_sums(step, at8):
        rcv8 = rcv[at8]
        for h in range(BLK // SUB):
            at, lanes, first = sub(step, h)
            mhe = (mask_of(count[0], first, SUB) * he[at].astype(F32)).astype(BF)
            acc[...] += mm(hot_rows(rcv8[lanes], 0, NF), mhe)

    by_block(he_sums)
    ssum[...] = jnp.zeros_like(ssum)
    both(cland, cgs.at[0], cgr.at[0], (r, g))

    def give_q(k):
        return remote(q_own, q_all.at[rows(g, NC)], qs.at[0], qr.at[0], grp(k))

    over(NG, lambda k: give_q(k).start())

    gy = gz[...].astype(F32) + mm(table, gc[...])
    gyb = gy.astype(BF)
    gun = mm_nt(gyb, nout[...]) * dsn[...].astype(F32)
    gunb = gun.astype(BF)
    gagg[...] = mm_nt(gunb, nin[H:]).astype(BF)
    gagg_w[...] = mm_nt(gagg[...], eout[...]).astype(BF)
    wbuf[768:1024] = (wacc[3 * H :] + mm_tn(acc[...].astype(BF), gagg[...])).astype(BF)
    gyn[...] = gy + mm_nt(gunb, nin[0:H])
    wbuf[1024:1280] = mm_tn(nf[...], gunb).astype(BF)
    wbuf[1280:1536] = mm_tn(agg[...], gunb).astype(BF)
    wbuf[1536:1792] = mm_tn(hn[...], gyb).astype(BF)
    bias0[1:2] = jnp.sum(gun, axis=0, keepdims=True)
    early.start_one()


    def backward(step, at8):
        rcv_t = jnp.transpose(rcv[at8])
        for h in range(BLK // SUB):
            at, lanes, first = sub(step, h)
            m = mask_of(count[0], first, SUB)
            gue = (gue0[at] + m * mm(hot_cols(rcv_t[:, lanes], 0, NF), gagg_w[...])) * ds[at].astype(F32)
            gueb = gue.astype(BF)
            gueb_s[at] = gueb
            wacc[0:H] += mm_tn(ef[at], gueb)
            wacc[H : 2 * H] += mm_tn(xs[at], gueb)
            wacc[2 * H : 3 * H] += mm_tn(xr[at], gueb)
            bias0[0:1] += jnp.sum(gue, axis=0, keepdims=True)

    by_block(backward)
    wbuf[0 : 3 * H] = wacc[0 : 3 * H].astype(BF)
    late.start_one()

    def one_bias(k):
        return remote(bias0, bl1.at[g], c1s.at[0], c1r.at[0], grp(k))

    def two_bias(k):
        return remote(bias1, bl2.at[r], c2s.at[0], c2r.at[0], row(k))

    bl1[g] = bias0[...]
    over(NG, lambda k: one_bias(k).start())

    def keep_def(step):
        at = pl.ds(pl.multiple_of(step * BLK, BLK), BLK)
        return pltpu.make_async_copy(defb.at[at], def_out.at[at], outs.at[EF // BLK + step])

    def hooked(hooks, step, h):
        for (at_step, at_h), then in hooks:
            if at_h == h:
                pl.when(step == at_step)(then)

    scatter_hooks = (((0, 1), early.start_two), ((1, 1), late.start_two), ((1, 1), early.start_three))

    def scatter(step, at8):
        snd8, rcv8 = snd[at8], rcv[at8]
        for h in range(BLK // SUB):
            hooked(scatter_hooks, step, h)
            at, lanes, _ = sub(step, h)
            gueb = gueb_s[at]
            ssum[0:NX] += mm(hot_rows(snd8[lanes], 0, NX), gueb)
            ssum[NX:] += mm(hot_rows(rcv8[lanes], 0, NF), gueb)

    widen_hooks = (((0, 1), late.start_three), ((1, 1), early.start_four))

    def edge_grads(step, at8):
        rcv_t = jnp.transpose(rcv[at8])
        for h in range(BLK // SUB):
            hooked(widen_hooks, step, h)
            at, lanes, first = sub(step, h)
            m = mask_of(count[0], first, SUB)
            gen = ge[at].astype(F32) + m * mm(hot_cols(rcv_t[:, lanes], 0, NF), gagg[...])
            defb[at] = (gen + mm_nt(gueb_s[at], ein[0:H])).astype(BF)
        keep_def(step).start()

    by_block(scatter)
    sums_b = ssum[...].astype(BF)
    dh[...] = mm_nt(sums_b[NF:NX], ein[H : 2 * H]).astype(BF)
    back = swap_halo(dh, hland, hs, hr, -1)
    for b in back:
        b.start()
    by_block(edge_grads)
    gyn[...] += mm_nt(sums_b[0:NF], ein[H : 2 * H]) + mm_nt(sums_b[NX:], ein[2 * H :])
    both(cland, qs.at[0], qr.at[0], (r, g))
    ptable = hot_cols(jnp.transpose(ct[...]), 0, GC, jnp.transpose(pw[...].astype(F32)))
    y[...] += mm(ptable, mm(q_all[...], prol[...]).astype(BF))
    last = 2 * (EF // BLK)
    keep_nr = pltpu.make_async_copy(y, nr_out, outs.at[last])
    keep_nr.start()
    late.start_four()
    both(bl1.at[pl.ds(0, NG - 1)], c1s.at[0], c1r.at[0], (r, g))
    total = bl1[0]
    for k in range(1, NG):
        total += bl1[k]
    bias1[...] = total
    bl2[r] = total
    over(NR, lambda k: two_bias(k).start())
    both(hland, hs.at[0], hr.at[0], (r, g))
    blank_outside(hland, 1)
    gyn[...] += mm_tn(halo_pick(hidx[...], 0, NF), hland[...])
    keep_dn = pltpu.make_async_copy(gyn, dn_out, outs.at[last + 1])
    keep_dn.start()
    both(bl2.at[pl.ds(0, NR - 1)], c2s.at[0], c2r.at[0], (r, g))
    total = bl2[0]
    for k in range(1, NR):
        total += bl2[k]
    b_out[...] = total
    early.finish()
    keep_b = pltpu.make_async_copy(b_out, b_hbm, outs.at[last + 2])
    keep_b.start()
    early_rows, late_rows = pl.ds(W_LATE, W_EARLY), pl.ds(0, W_LATE)
    keep_early = pltpu.make_async_copy(w_out.at[early_rows], w_hbm.at[early_rows], outs.at[last + 3])
    keep_early.start()
    for step in range(EF // BLK):
        keep_en(step).wait()
        keep_def(step).wait()
    keep_nr.wait()
    keep_dn.wait()
    late.finish()
    keep_late = pltpu.make_async_copy(w_out.at[late_rows], w_hbm.at[late_rows], outs.at[last + 4])
    keep_late.start()
    keep_b.wait()
    keep_early.wait()
    keep_late.wait()


SIZES = (768, 256, 512, 256, 256, 256, 256)
CHUNK = 2048


def result_kernel(b_h, nr_h, dn_h, de_h, en_h, w_h, *refs):
    biases, big, mats = refs[0:3], refs[3:7], refs[7:14]
    nr, dn, de, en, w, wide_de, wide_en, wide_w, b, *lines, in_sem, out_sem = refs[14:]
    chunks = [pl.ds(c * CHUNK, CHUNK) for c in range(EF // CHUNK)]
    arriving, leaving = [], []

    def bring(src, dst):
        arriving.append(pltpu.make_async_copy(src, dst, in_sem.at[len(arriving)]))
        arriving[-1].start()
        return arriving[-1]

    def leave(src, dst):
        leaving.append(pltpu.make_async_copy(src, dst, out_sem.at[len(leaving)]))
        leaving[-1].start()

    edges = []
    for at in chunks:
        for src, mid, wide, dst in ((en_h, en, wide_en, big[0]), (de_h, de, wide_de, big[1])):
            edges.append((bring(src.at[at], mid.at[at]), mid, wide, dst, at))
    nodes = [(bring(src, mid), mid, dst) for src, mid, dst in ((nr_h, nr, big[2]), (dn_h, dn, big[3]))]
    b_here = bring(b_h, b)
    w_here = bring(w_h, w)
    for here_, mid, wide, dst, at in edges:
        here_.wait()
        wide[at] = mid[at].astype(F32)
        leave(wide.at[at], dst.at[at])
    for here_, mid, dst in nodes:
        here_.wait()
        leave(mid, dst)
    b_here.wait()
    for i, (line, dst) in enumerate(zip(lines, biases)):
        line[...] = b[i : i + 1].reshape(H)
        leave(line, dst)
    w_here.wait()
    first = 0
    for dst, size in zip(mats, SIZES):
        wide_w[first : first + size] = w[first : first + size].astype(F32)
        leave(wide_w.at[pl.ds(first, size)], dst)
        first += size
    for c in leaving:
        c.wait()


def body(node_feat, edge_feat, senders, receivers, edge_count, halo_index, coarse_target,
         restrict_weight, prolong_weight, edge_in, edge_bias, edge_out, node_in, node_bias, node_out,
         coarse_in, coarse_bias, coarse_out, prolong, grad_nodes, grad_edges):
    snd = senders.reshape(EF // 128, 128)
    rcv = receivers.reshape(EF // 128, 128)
    ct = coarse_target.reshape(NF // 128, 128)
    rw = restrict_weight.reshape(NF // 128, 128)
    pw = prolong_weight.reshape(NF // 128, 128)
    hidx = halo_index.reshape(8, 32)

    def shape(dims, dtype=BF):
        return jax.ShapeDtypeStruct(dims, dtype)

    def sems(*sizes):
        return [pltpu.SemaphoreType.DMA((n,)) for n in sizes]

    def far(n):
        return [pl.BlockSpec(memory_space=pl.ANY)] * n

    def vmem(*dims, dtype=BF):
        return pltpu.VMEM(dims, dtype)

    blocks = EF // BLK
    w_all, b_all, nr, dn, de, en = pl.pallas_call(
        step_kernel,
        out_shape=[
            shape((WROWS, H)), shape((8, H), F32), shape((NF, H), F32), shape((NF, H), F32),
            shape((EF, H)), shape((EF, H)),
        ],
        in_specs=[pl.BlockSpec(memory_space=pltpu.SMEM)] + far(20),
        out_specs=far(6),
        scratch_shapes=[
            vmem(8, 32, dtype=I32), vmem(8, 128, dtype=I32), vmem(EF // 128, 128, dtype=I32),
            vmem(EF // 128, 128, dtype=I32),
        ]
        + sems(4)
        + [
            vmem(WROWS, H), vmem(8, H, dtype=F32),
            vmem(NF, H), vmem(NF, H), vmem(8, 128), vmem(768, H), vmem(EF, H), vmem(H), vmem(H, H),
            vmem(512, H), vmem(H), vmem(H, H), vmem(8, 128), vmem(H, H), vmem(H), vmem(H, H), vmem(H, H),
            vmem(EF, H),
        ]
        + sems(16)
        + [
            vmem(256, H), vmem(256, H), vmem(GC, H), vmem(NG - 1, NC, H), vmem(EF, H), vmem(EF, H),
            vmem(EF, H), vmem(EF, H), vmem(EF, H), vmem(NF, H, dtype=F32), vmem(NF, H),
        ]
        + [
            vmem(NF, H, dtype=F32), vmem(NF, H), vmem(NF, H), vmem(GC, H), vmem(NG - 1, NC, H),
            vmem(NC, H), vmem(GC, H), vmem(NC, H), vmem(GC, H), vmem(NF, H), vmem(NF, H), vmem(EF, H, dtype=F32), vmem(NF, H, dtype=F32),
            vmem(NT, H, dtype=F32), vmem(1024, H, dtype=F32), vmem(WROWS, H), vmem(EF, H), vmem(EF, H),
            vmem(256, H), vmem(256, H), vmem(8, H, dtype=F32), vmem(8, H, dtype=F32),
            vmem(NG, 8, H, dtype=F32), vmem(NR, 8, H, dtype=F32),
        ]
        + sems(*[1] * 16, 2 * blocks + 5)
        + Total.scratch(*EARLY)
        + Total.scratch(*LATE),
        compiler_params=pltpu.CompilerParams(
            collective_id=0, has_side_effects=True, vmem_limit_bytes=LIMIT * MIB
        ),
        name="step",
    )(edge_count, hidx, ct, snd, rcv, node_feat, grad_nodes, pw, edge_in, edge_feat, edge_bias, edge_out,
      node_in, node_bias, node_out, rw, coarse_in, coarse_bias, coarse_out, prolong, grad_edges)

    chunks = EF // CHUNK
    g_eb, g_nb, g_cb, edge_new, d_edge_feat, node_result, d_node_feat, *mats = pl.pallas_call(
        result_kernel,
        out_shape=[shape((H,), F32)] * 3 + [shape((n, H), F32) for n in (EF, EF, NF, NF) + SIZES],
        in_specs=far(6),
        out_specs=far(14),
        scratch_shapes=[
            vmem(NF, H, dtype=F32), vmem(NF, H, dtype=F32), vmem(EF, H), vmem(EF, H), vmem(WROWS, H),
            vmem(EF, H, dtype=F32), vmem(EF, H, dtype=F32), vmem(WROWS, H, dtype=F32),
            vmem(8, H, dtype=F32), *[vmem(H, dtype=F32)] * 3,
        ]
        + sems(2 * chunks + 4, 2 * chunks + 12),
        compiler_params=pltpu.CompilerParams(vmem_limit_bytes=LIMIT * MIB),
        name="results",
    )(b_all, nr, dn, de, en, w_all)
    g_ein, g_eout, g_nin, g_nout, g_cin, g_cout, g_pr = mats
    return (node_result, edge_new, d_node_feat, d_edge_feat, g_ein, g_eb, g_eout, g_nin, g_nb, g_nout,
            g_cin, g_cb, g_cout, g_pr)


def solution(mesh):
    wide = P(("row", "grp"), None)
    line = P(("row", "grp"))
    in_specs = (
        (wide, wide, line, line, line, P(("row", "grp"), None, None), line, line, line)
        + (P(),) * 10
        + (wide, wide)
    )
    out_specs = (wide,) * 4 + (P(),) * 10
    return jax.shard_map(body, mesh=mesh, in_specs=in_specs, out_specs=out_specs, check_vma=False)
```
